32 devices in a mesh: groups: 2 (over x), row: 4 (over y, core), col: 4 (over z).
Axes of the slice: x: 2, y: 2, z: 4, core: 2. Of those that a mesh axis runs over, the one named last changes fastest.
Arguments:
- operand_panel: bfloat16 [4096, 8192], P(('groups', 'row'), 'col'), parts along dimension 0
- slot_blocks: bfloat16 [128, 4, 128, 128], P(('groups', 'col'), 'row'), parts along dimension 0
- slot_columns: int32 [128, 4], P(('groups', 'col')), parts along dimension 0, may hold values from 0 to 15, as said below
- live_counts: int32 [128], P(('groups', 'col')), parts along dimension 0, may hold values from 1 to 4, as said below
Outputs:
- mcl_columns: float32 [4096, 2048], P(('groups', 'row'), 'col'), parts along dimension 0
- column_load: int32 [32], P(('groups', 'col')), parts along dimension 0
The draws below stay inside these ranges and needn't reach their ends.
There are 2 independent parts, one for each index of `groups`. The reference program is written for one: setup_inputs(seed, part) draws one part's arguments, and reference() takes and returns one part's arrays. A program takes and returns all parts, laid end to end along the dimension named above; each array names one. Nothing has to cross between parts.
Inputs may be any that keep to these rules, and one draw needn't show every extreme that they name: `slot_columns`: within each contraction block row the 4 slots name distinct block columns; values of slots that are not live are present but carry no block. A slot e of block row k is live exactly when ((e - k) mod 4) < live_counts[k].
All inputs are finite; a program needn't handle non-finite values.
Results may differ from the reference program's by a relative error of at most 0.0003.
Values may be sent and summed in bfloat16 or wider, within the bound.
No kernel may reach another device: no remote copies, remote signals or barrier semaphores. Data moves between devices by JAX's collectives and lax.ppermute only.
A program may use at most 128 MiB of HBM per device.

```python
import math
import jax
import jax.numpy as jnp

B = 128
NR = 16
KB = 64
SLAB = 16
NZ = 4


def draw_operand_panel(key, part):
    key = jax.random.fold_in(key, 11)
    first, second = jax.random.split(key, 2)
    shape = (NR * B, KB * B)
    place = jnp.arange(NR * B, dtype=jnp.float32) / (NR * B)
    base = jnp.abs(jax.random.normal(first, shape, jnp.float32))
    trend = jnp.exp(place * math.log(3.0))
    spread = jnp.exp(jax.random.uniform(second, (NR * B,), jnp.float32) * math.log(10.0))
    values = base * (spread * trend)[:, None] * (KB * B) ** (-0.5)
    return values.astype(jnp.bfloat16)


def draw_slot_blocks(key, part):
    key = jax.random.fold_in(key, 23)
    first, second = jax.random.split(key)
    shape = (KB, NZ, B, B)
    base = jnp.abs(jax.random.normal(first, shape, jnp.float32))
    spread = jnp.exp(jax.random.uniform(second, (KB, 1, 1, 1), jnp.float32) * math.log(10.0))
    return (base * spread * B ** (-0.5)).astype(jnp.bfloat16)


def draw_slot_columns(key, part):
    key = jax.random.fold_in(key, 37)
    first, second, third, fourth = jax.random.split(key, 4)
    keys = jax.random.split(first, KB)
    columns = jax.vmap(lambda one: jax.random.permutation(one, SLAB)[:NZ])(keys).astype(jnp.int32)
    upper = (SLAB - 1 - jax.random.permutation(second, NZ)).astype(jnp.int32)
    lower = jax.random.permutation(third, NZ).astype(jnp.int32)
    where_upper = jax.random.randint(fourth, (), 0, KB)
    where_lower = jnp.mod(where_upper + 1, KB)
    columns = columns.at[where_upper].set(upper)
    columns = columns.at[where_lower].set(lower)
    return columns


def draw_live_counts(key, part):
    key = jax.random.fold_in(key, 41)
    first, second, third = jax.random.split(key, 3)
    counts = jax.random.randint(first, (KB,), NZ // 4, NZ + 1).astype(jnp.int32)
    where_most = jax.random.randint(second, (), 0, KB)
    where_least = jnp.mod(where_most + 1 + jax.random.randint(third, (), 0, KB - 1), KB)
    counts = counts.at[where_most].set(NZ)
    counts = counts.at[where_least].set(NZ // 4)
    return counts


def setup_inputs(seed: int = 0, part: int = 0) -> dict:
    key_list = jax.random.split(jax.random.key(seed), 5)
    part_splits = jax.random.split(jax.random.fold_in(key_list[4], part), 5)
    operand_panel = draw_operand_panel(jax.random.fold_in(jax.random.fold_in(key_list[4], part), 71), part)
    slot_blocks = draw_slot_blocks(jax.random.fold_in(jax.random.fold_in(key_list[4], part), 71), part)
    slot_columns = draw_slot_columns(jax.random.fold_in(jax.random.fold_in(key_list[4], part), 71), part)
    live_counts = draw_live_counts(jax.random.fold_in(jax.random.fold_in(key_list[4], part), 71), part)
    return {"operand_panel": operand_panel, "slot_blocks": slot_blocks, "slot_columns": slot_columns, "live_counts": live_counts}


def reference(operand_panel, slot_blocks, slot_columns, live_counts):
    places = jnp.arange(NZ, dtype=jnp.int32)
    rows_index = jnp.arange(KB, dtype=jnp.int32)
    live = jnp.mod(places[None, :] - rows_index[:, None], NZ) < live_counts[:, None]
    onehot = (slot_columns[:, :, None] == jnp.arange(SLAB, dtype=jnp.int32)[None, None, :]) & live[:, :, None]
    onehot_f = onehot.astype(jnp.float32)
    right_slab = jnp.einsum('kej,kebc->kbjc', onehot_f, slot_blocks.astype(jnp.float32))
    right_slab = right_slab.astype(jnp.bfloat16).reshape(KB * B, SLAB * B)
    expanded = jnp.dot(operand_panel, right_slab, preferred_element_type=jnp.float32)
    inflated = expanded * expanded
    totals = jnp.sum(inflated, axis=0)
    mcl_columns = inflated / (totals / (NR * B) + 1e-6)
    column_load = jnp.sum(onehot_f, axis=(0, 1)).astype(jnp.int32)
    return mcl_columns, column_load
```

```python
import functools

import jax
import jax.numpy as jnp
from jax import lax
from jax.experimental import pallas as pl
from jax.experimental.pallas import tpu as pltpu
from jax.sharding import PartitionSpec as P

SLAB_DEV = 4
SIDE = 128
HEAD = 16
TILE = 256
STEPS = 32752.0
OCTAVE = 128.0

VMEM = pl.BlockSpec(memory_space=pltpu.VMEM)
SMEM = pl.BlockSpec(memory_space=pltpu.SMEM)


def code_scale(values):
    most = jnp.max(jnp.abs(values), axis=0, keepdims=True)
    octaves = jnp.log2(jnp.maximum(most, 1e-30))
    return jnp.ceil(octaves * OCTAVE)


def encode(values, code):
    scaled = jnp.round(values * (STEPS * jnp.exp2(code * (-1.0 / OCTAVE))))
    return jnp.clip(scaled, -32767.0, 32767.0).astype(jnp.int32).astype(jnp.int16)


def head_rows(code, counts):
    shape = (HEAD, code.shape[1])
    row = lax.broadcasted_iota(jnp.int32, shape, 0)
    code = jnp.broadcast_to(code.astype(jnp.int32), shape)
    counts = jnp.broadcast_to(counts, shape)
    return jnp.where(row == 0, code, jnp.where(row == 1, counts, 0)).astype(jnp.int16)


def put_coded(out, lanes, values, counts):
    code = code_scale(values)
    out[pl.ds(0, HEAD), lanes] = head_rows(code, counts)
    out[pl.ds(HEAD, values.shape[0]), lanes] = encode(values, code)


def decode(ref, lanes):
    rows = ref.shape[0] - HEAD
    head = ref[pl.ds(0, HEAD), lanes].astype(jnp.int32).astype(jnp.float32)
    scale = jnp.exp2(head[0:1] * (1.0 / OCTAVE)) * (1.0 / STEPS)
    return ref[pl.ds(HEAD, rows), lanes].astype(jnp.int32).astype(jnp.float32) * scale


def head_counts(ref, lanes):
    return ref[pl.ds(0, HEAD), lanes].astype(jnp.int32)[1:2]


def slot_of(place, ny):
    me = lax.axis_index("row")
    y, core = lax.div(me, 2), lax.rem(me, 2)
    return lax.rem(y + ny - place // 2, ny) * 2 + (core if place % 2 == 0 else 1 - core)


def is_live(columns, counts, k, e):
    rows, slots = columns.shape
    row_index = lax.axis_index("col") * rows + k
    all_rows = rows * lax.axis_size("col")
    return lax.rem(e - row_index + all_rows * slots, slots) < counts[k]


def fill(slab, shard, columns, counts, blocks):
    rows, _ = columns.shape
    slab[...] = jnp.zeros_like(slab)
    for place, held in enumerate(blocks):
        e = slot_of(place, len(blocks) // 2)

        def one(k, carry, held=held, e=e):
            column = columns[k, e] - shard * SLAB_DEV

            @pl.when(is_live(columns, counts, k, e) & (column >= 0) & (column < SLAB_DEV))
            def _():
                at = (pl.ds(pl.multiple_of(k * SIDE, SIDE), SIDE), pl.ds(pl.multiple_of(column * SIDE, SIDE), SIDE))
                slab[at] = held[k, 0]

            return carry

        lax.fori_loop(0, rows, one, 0, unroll=False)


def count_live(load, columns, counts):
    rows, slots = columns.shape

    def clear(j, carry):
        load[j] = 0
        return carry

    lax.fori_loop(0, load.shape[0], clear, 0)

    def one(k, carry):
        for e in range(slots):
            j = columns[k, e]
            load[j] = load[j] + is_live(columns, counts, k, e).astype(jnp.int32)
        return carry

    lax.fori_loop(0, rows, one, 0)


def counts_of(load, shard, tile):
    lane = lax.broadcasted_iota(jnp.int32, (1, TILE), 1)
    counts = jnp.zeros((1, TILE), jnp.int32)
    for j in range(TILE // SIDE):
        block = shard * SLAB_DEV + tile * (TILE // SIDE) + j
        counts = jnp.where((lane >= j * SIDE) & (lane < (j + 1) * SIDE), load[block], counts)
    return counts


def tiles(width, body):
    def step(tile, carry):
        body(tile, pl.ds(pl.multiple_of(tile * TILE, TILE), TILE))
        return carry

    lax.fori_loop(0, width // TILE, step, 0)


def coded_product(which, nblocks, *refs):
    columns, counts, operand, *blocks = refs[: 3 + nblocks]
    out, slab, load = refs[3 + nblocks :]
    shard = which(lax.axis_index("col"))
    count_live(load, columns, counts)
    fill(slab, shard, columns, counts, blocks)

    def body(tile, lanes):
        values = jnp.dot(operand[...], slab[:, lanes], preferred_element_type=jnp.float32)
        put_coded(out, lanes, values, counts_of(load, shard, tile))

    tiles(slab.shape[1], body)


def plain_products(which, nblocks, *refs):
    columns, counts, operand, *blocks = refs[: 3 + nblocks]
    outs = refs[3 + nblocks : 3 + nblocks + len(which)]
    loads = refs[3 + nblocks + len(which) : 3 + nblocks + 2 * len(which)]
    slab, load = refs[3 + nblocks + 2 * len(which) :]
    count_live(load, columns, counts)
    for one, out, row in zip(which, outs, loads):
        shard = one(lax.axis_index("col"))
        fill(slab, shard, columns, counts, blocks)

        def body(tile, lanes, out=out, row=row, shard=shard):
            out[:, lanes] = jnp.dot(operand[...], slab[:, lanes], preferred_element_type=jnp.float32)
            row[:, lanes] = jnp.broadcast_to(counts_of(load, shard, tile), (8, TILE))

        tiles(slab.shape[1], body)


def relay(own, own_load, came, out):
    place = lax.axis_index("col")
    inner = (place == 1) | (place == 2)

    def body(tile, lanes):
        @pl.when(inner)
        def _():
            put_coded(out, lanes, own[:, lanes] + decode(came, lanes), own_load[0:1, lanes] + head_counts(came, lanes))

        @pl.when(jnp.logical_not(inner))
        def _():
            put_coded(out, lanes, own[:, lanes], own_load[0:1, lanes])

    tiles(own.shape[1], body)


def settle(own, own_load, came_a, came_b, came_f, out, out_load):
    place = lax.axis_index("col")
    inner = (place == 1) | (place == 2)

    def body(tile, lanes):
        @pl.when(inner)
        def _():
            out[:, lanes] = own[:, lanes] + decode(came_b, lanes) + decode(came_f, lanes)
            load = own_load[0:1, lanes] + head_counts(came_b, lanes) + head_counts(came_f, lanes)
            out_load[:, lanes] = jnp.broadcast_to(load, (8, TILE))

        @pl.when(jnp.logical_not(inner))
        def _():
            out[:, lanes] = own[:, lanes] + decode(came_a, lanes)
            out_load[:, lanes] = jnp.broadcast_to(own_load[0:1, lanes] + head_counts(came_a, lanes), (8, TILE))

    tiles(own.shape[1], body)


def inflate(own, own_load, came, out, totals, load):
    def body(tile, lanes):
        expanded = own[:, lanes] + decode(came, lanes)
        inflated = expanded * expanded
        out[:, lanes] = inflated
        totals[:, lanes] = jnp.sum(inflated.reshape(-1, 8, TILE), axis=0)

    tiles(own.shape[1], body)
    for j in range(SLAB_DEV):
        lanes = pl.ds(j * SIDE, SIDE)
        load[j] = jnp.max(own_load[0:1, lanes] + head_counts(came, lanes))


def scale(all_rows, inflated, *refs):
    *totals, out = refs

    def body(tile, lanes):
        total = totals[0][:, lanes]
        for other in totals[1:]:
            total = total + other[:, lanes]
        total = jnp.sum(total, axis=0, keepdims=True)
        out[:, lanes] = inflated[:, lanes] * (1.0 / (total / all_rows + 1e-06))

    tiles(inflated.shape[1], body)


def call(kernel, ins, out_shape, out_specs, scratch=(), flops=0):
    moved = sum(x.size * x.dtype.itemsize for x in list(ins) + list(out_shape))
    return pl.pallas_call(
        kernel,
        in_specs=[SMEM if x.dtype == jnp.int32 and x.ndim < 3 and x.size <= 4096 and x.shape[-1] <= 32 else VMEM for x in ins],
        out_shape=out_shape,
        out_specs=out_specs,
        scratch_shapes=list(scratch),
        compiler_params=pltpu.CompilerParams(vmem_limit_bytes=40 << 20),
        cost_estimate=pl.CostEstimate(flops=flops, bytes_accessed=moved, transcendentals=0),
    )(*ins)


def body_line(operand_panel, slot_blocks, slot_columns, live_counts):
    ny = lax.axis_size("row") // 2
    rows, depth = operand_panel.shape
    width = SLAB_DEV * SIDE
    slab_width = SLAB_DEV * lax.axis_size("col")
    f32 = functools.partial(jax.ShapeDtypeStruct, dtype=jnp.float32)
    i32 = functools.partial(jax.ShapeDtypeStruct, dtype=jnp.int32)
    coded = jax.ShapeDtypeStruct((HEAD + rows, width), jnp.int16)

    swap = [(a, a ^ 1) for a in range(2 * ny)]

    def turn(by):
        return [(a, ((a // 2 + by) % ny) * 2 + a % 2) for a in range(2 * ny)]

    held = [slot_blocks] + [lax.ppermute(slot_blocks, "row", turn(by)) for by in range(1, ny)]
    blocks = [x for mine in held for x in (mine, lax.ppermute(mine, "row", swap))]

    ins = [slot_columns, live_counts, operand_panel, *blocks]
    scratch = [pltpu.VMEM((depth, width), jnp.bfloat16), pltpu.SMEM((slab_width,), jnp.int32)]
    flops = 2 * rows * depth * width

    def first(z):
        return jnp.where(lax.rem(z, 2) == 0, 3, 0)

    def second(z):
        return jnp.where(z < 2, 2, 1)

    def third(z):
        return jnp.where(z == 0, 1, jnp.where(z == 1, 3, jnp.where(z == 2, 0, 2)))

    def product(which):
        return call(functools.partial(coded_product, which, len(blocks)), ins, [coded], [VMEM], scratch, flops)[0]

    send_a = product(first)
    came_a = lax.ppermute(send_a, "col", [(0, 1), (1, 0), (2, 3), (3, 2)])
    send_b = product(second)
    came_b = lax.ppermute(send_b, "col", [(1, 2), (2, 1)])
    came_f = lax.ppermute(send_b, "col", [(0, 2), (3, 1)])
    passed, own, passed_load, own_load = call(
        functools.partial(plain_products, (third, lambda z: z), len(blocks)),
        ins,
        [f32((rows, width)), f32((rows, width)), i32((8, width)), i32((8, width))],
        [VMEM] * 4,
        scratch,
        2 * flops,
    )
    [send_t] = call(relay, [passed, passed_load, came_a], [coded], [VMEM])
    came_t = lax.ppermute(send_t, "col", [(0, 1), (1, 3), (3, 2), (2, 0)])
    own, own_load = call(
        settle, [own, own_load, came_a, came_b, came_f], [f32((rows, width)), i32((8, width))], [VMEM] * 2
    )
    inflated, totals, load = call(
        inflate, [own, own_load, came_t], [f32((rows, width)), f32((8, width)), i32((SLAB_DEV,))], [VMEM, VMEM, SMEM]
    )
    others = [totals]
    for by in range(ny):
        for flip in (0, 1):
            if by or flip:
                pairs = [(a, ((a // 2 + by) % ny) * 2 + (a % 2 ^ flip)) for a in range(2 * ny)]
                others.append(lax.ppermute(totals, "row", pairs))
    all_rows = rows * lax.axis_size("row")
    [mcl_columns] = call(
        functools.partial(scale, all_rows), [inflated, *others], [f32((rows, width))], [VMEM]
    )
    return mcl_columns, load


def densify(blocks, columns, counts, first_row, slab_width):
    rows_here, slots = columns.shape
    side = blocks.shape[2]
    places = jnp.arange(slots, dtype=jnp.int32)
    rows_index = first_row + jnp.arange(rows_here, dtype=jnp.int32)
    live = jnp.mod(places[None, :] - rows_index[:, None], slots) < counts[:, None]
    onehot = (columns[:, :, None] == jnp.arange(slab_width, dtype=jnp.int32)[None, None, :]) & live[:, :, None]
    dense = jnp.einsum(
        "kej,kebc->kbjc", onehot.astype(jnp.bfloat16), blocks, preferred_element_type=jnp.float32
    )
    dense = dense.astype(jnp.bfloat16).reshape(rows_here * side, slab_width * side)
    return (dense, jnp.sum(onehot.astype(jnp.float32), axis=(0, 1)))


def body_any(operand_panel, slot_blocks, slot_columns, live_counts):
    gathered = lax.all_gather(slot_blocks, "row", axis=1, tiled=True)
    slab_width = SLAB_DEV * lax.axis_size("col")
    first_row = lax.axis_index("col") * slot_columns.shape[0]
    dense, load = densify(gathered, slot_columns, live_counts, first_row, slab_width)
    partial_terms = jnp.dot(operand_panel, dense, preferred_element_type=jnp.float32)
    expanded, load_mine = (
        lax.psum_scatter(partial_terms, "col", scatter_dimension=1, tiled=True),
        lax.psum_scatter(load, "col", scatter_dimension=0, tiled=True),
    )
    inflated = expanded * expanded
    totals = lax.psum(jnp.sum(inflated, axis=0), "row")
    all_rows = expanded.shape[0] * lax.axis_size("row")
    mcl_columns = inflated / (totals / all_rows + 1e-06)
    return (mcl_columns, load_mine.astype(jnp.int32))


def solution(mesh):
    placed = (
        P(("groups", "row"), "col"),
        P(("groups", "col"), "row", None, None),
        P(("groups", "col"), None),
        P(("groups", "col")),
    )
    return jax.shard_map(
        body_line if mesh.shape["col"] == 4 else body_any,
        mesh=mesh,
        in_specs=placed,
        out_specs=(P(("groups", "row"), "col"), P(("groups", "col"))),
        check_vma=False,
    )
```

```python
import functools

import jax
import jax.numpy as jnp
from jax import lax
from jax.experimental import pallas as pl
from jax.experimental.pallas import tpu as pltpu
from jax.sharding import PartitionSpec as P

SLAB_DEV = 4
SIDE = 128
HEAD = 16
TILE = 256
STEPS = 32752.0
OCTAVE = 128.0

VMEM = pl.BlockSpec(memory_space=pltpu.VMEM)
SMEM = pl.BlockSpec(memory_space=pltpu.SMEM)


def code_scale(values):
    most = jnp.max(jnp.abs(values), axis=0, keepdims=True)
    octaves = jnp.log2(jnp.maximum(most, 1e-30))
    return jnp.ceil(octaves * OCTAVE)


def encode(values, code):
    scaled = jnp.round(values * (STEPS * jnp.exp2(code * (-1.0 / OCTAVE))))
    return jnp.clip(scaled, -32767.0, 32767.0).astype(jnp.int32).astype(jnp.int16)


def head_rows(code, counts):
    shape = (HEAD, code.shape[1])
    row = lax.broadcasted_iota(jnp.int32, shape, 0)
    code = jnp.broadcast_to(code.astype(jnp.int32), shape)
    counts = jnp.broadcast_to(counts, shape)
    return jnp.where(row == 0, code, jnp.where(row == 1, counts, 0)).astype(jnp.int16)


def put_coded(out, lanes, values, counts):
    code = code_scale(values)
    out[pl.ds(0, HEAD), lanes] = head_rows(code, counts)
    out[pl.ds(HEAD, values.shape[0]), lanes] = encode(values, code)


def decode(ref, lanes):
    rows = ref.shape[0] - HEAD
    head = ref[pl.ds(0, HEAD), lanes].astype(jnp.int32).astype(jnp.float32)
    scale = jnp.exp2(head[0:1] * (1.0 / OCTAVE)) * (1.0 / STEPS)
    return ref[pl.ds(HEAD, rows), lanes].astype(jnp.int32).astype(jnp.float32) * scale


def head_counts(ref, lanes):
    return ref[pl.ds(0, HEAD), lanes].astype(jnp.int32)[1:2]


def slot_of(place, ny):
    me = lax.axis_index("row")
    y, core = lax.div(me, 2), lax.rem(me, 2)
    return lax.rem(y + ny - place // 2, ny) * 2 + (core if place % 2 == 0 else 1 - core)


def is_live(columns, counts, k, e):
    slots, rows = columns.shape
    row_index = lax.axis_index("col") * rows + k
    all_rows = rows * lax.axis_size("col")
    return lax.rem(e - row_index + all_rows * slots, slots) < counts[k]


def sort_live(ny, columns, counts, operand, own, lists, lens, load, operand_near, own_near, sems):
    copies = [
        pltpu.make_async_copy(far, near, sems.at[j])
        for j, (far, near) in enumerate(((operand, operand_near), (own, own_near)))
    ]
    for copy in copies:
        copy.start()
    slots, rows = columns.shape
    shards = load.shape[0] // SLAB_DEV

    def clear(ref):
        def step(j, carry):
            ref[j] = 0
            return carry

        lax.fori_loop(0, ref.shape[0], step, 0)

    clear(lens)
    clear(load)
    for place in range(slots):
        e = slot_of(place, ny)

        def one(k, carry, place=place, e=e):
            @pl.when(is_live(columns, counts, k, e))
            def _():
                column = columns[e, k]
                load[column] = load[column] + 1
                shard = lax.div(column, SLAB_DEV)
                at = place * shards + shard
                length = lens[at]
                lists[at * rows + length] = k * SLAB_DEV + column - shard * SLAB_DEV
                lens[at] = length + 1

            return carry

        lax.fori_loop(0, rows, one, 0)
    for copy in copies:
        copy.wait()


def fill(slab, shard, lists, lens, blocks):
    rows = blocks[0].shape[0]
    shards = lens.shape[0] // len(blocks)
    slab[...] = jnp.zeros_like(slab)
    for place, held in enumerate(blocks):
        at = place * shards + shard

        def one(j, carry, held=held, at=at):
            entry = lists[at * rows + j]
            k, column = lax.div(entry, SLAB_DEV), lax.rem(entry, SLAB_DEV)
            where = (pl.ds(pl.multiple_of(k * SIDE, SIDE), SIDE), pl.ds(pl.multiple_of(column * SIDE, SIDE), SIDE))
            slab[where] = held[k, 0]
            return carry

        lax.fori_loop(0, lens[at], one, 0)


def counts_of(load, shard, tile):
    lane = lax.broadcasted_iota(jnp.int32, (1, TILE), 1)
    counts = jnp.zeros((1, TILE), jnp.int32)
    for j in range(TILE // SIDE):
        block = shard * SLAB_DEV + tile * (TILE // SIDE) + j
        counts = jnp.where((lane >= j * SIDE) & (lane < (j + 1) * SIDE), load[block], counts)
    return counts


def tiles(width, body):
    def step(tile, carry):
        body(tile, pl.ds(pl.multiple_of(tile * TILE, TILE), TILE))
        return carry

    lax.fori_loop(0, width // TILE, step, 0)


def coded_products(which, nblocks, *refs):
    lists, lens, load, operand, *blocks = refs[: 4 + nblocks]
    outs = refs[4 + nblocks : 4 + nblocks + len(which)]
    slab = refs[-1]
    for one, out in zip(which, outs):
        shard = one(lax.axis_index("col"))
        fill(slab, shard, lists, lens, blocks)

        def body(tile, lanes, out=out, shard=shard):
            values = jnp.dot(operand[...], slab[:, lanes], preferred_element_type=jnp.float32)
            put_coded(out, lanes, values, counts_of(load, shard, tile))

        tiles(slab.shape[1], body)


def plain_products(which, nblocks, *refs):
    lists, lens, load, operand, *blocks = refs[: 4 + nblocks]
    outs = refs[4 + nblocks : 4 + nblocks + len(which)]
    rows_out = refs[4 + nblocks + len(which) : 4 + nblocks + 2 * len(which)]
    slab = refs[-1]
    for one, out, row in zip(which, outs, rows_out):
        shard = one(lax.axis_index("col"))
        fill(slab, shard, lists, lens, blocks)

        def body(tile, lanes, out=out, row=row, shard=shard):
            out[:, lanes] = jnp.dot(operand[...], slab[:, lanes], preferred_element_type=jnp.float32)
            row[:, lanes] = jnp.broadcast_to(counts_of(load, shard, tile), (8, TILE))

        tiles(slab.shape[1], body)


def relay(own, own_load, came, out):
    place = lax.axis_index("col")
    inner = (place == 1) | (place == 2)

    def body(tile, lanes):
        @pl.when(inner)
        def _():
            put_coded(out, lanes, own[:, lanes] + decode(came, lanes), own_load[0:1, lanes] + head_counts(came, lanes))

        @pl.when(jnp.logical_not(inner))
        def _():
            put_coded(out, lanes, own[:, lanes], own_load[0:1, lanes])

    tiles(own.shape[1], body)


def settle(own, own_load, came_a, came_b, came_f, out, out_load):
    place = lax.axis_index("col")
    inner = (place == 1) | (place == 2)

    def body(tile, lanes):
        @pl.when(inner)
        def _():
            out[:, lanes] = own[:, lanes] + decode(came_b, lanes) + decode(came_f, lanes)
            load = own_load[0:1, lanes] + head_counts(came_b, lanes) + head_counts(came_f, lanes)
            out_load[:, lanes] = jnp.broadcast_to(load, (8, TILE))

        @pl.when(jnp.logical_not(inner))
        def _():
            out[:, lanes] = own[:, lanes] + decode(came_a, lanes)
            out_load[:, lanes] = jnp.broadcast_to(own_load[0:1, lanes] + head_counts(came_a, lanes), (8, TILE))

    tiles(own.shape[1], body)


def inflate(own, own_load, came, out, totals, load):
    def body(tile, lanes):
        expanded = own[:, lanes] + decode(came, lanes)
        inflated = expanded * expanded
        out[:, lanes] = inflated
        totals[:, lanes] = jnp.sum(inflated.reshape(-1, 8, TILE), axis=0)

    tiles(own.shape[1], body)
    for j in range(SLAB_DEV):
        lanes = pl.ds(j * SIDE, SIDE)
        load[j] = jnp.max(own_load[0:1, lanes] + head_counts(came, lanes))


def scale(all_rows, inflated, *refs):
    *totals, out = refs

    def body(tile, lanes):
        total = totals[0][:, lanes]
        for other in totals[1:]:
            total = total + other[:, lanes]
        total = jnp.sum(total, axis=0, keepdims=True)
        out[:, lanes] = inflated[:, lanes] * (1.0 / (total / all_rows + 1e-06))

    tiles(inflated.shape[1], body)


def call(kernel, ins, out_shape, out_specs, scratch=(), flops=0, few=0, space=VMEM):
    moved = sum(x.size * x.dtype.itemsize for x in list(ins) + list(out_shape))
    return pl.pallas_call(
        kernel,
        in_specs=[SMEM] * few + [space] * (len(ins) - few),
        out_shape=out_shape,
        out_specs=out_specs,
        scratch_shapes=list(scratch),
        compiler_params=pltpu.CompilerParams(vmem_limit_bytes=24 << 20),
        cost_estimate=pl.CostEstimate(flops=flops, bytes_accessed=moved, transcendentals=0),
    )(*ins)


def body_line(operand_panel, slot_blocks, slot_columns, live_counts):
    ny = lax.axis_size("row") // 2
    rows, depth = operand_panel.shape
    here, slots = slot_columns.shape
    width = SLAB_DEV * SIDE
    shards = lax.axis_size("col")
    f32 = functools.partial(jax.ShapeDtypeStruct, dtype=jnp.float32)
    i32 = functools.partial(jax.ShapeDtypeStruct, dtype=jnp.int32)
    coded = jax.ShapeDtypeStruct((HEAD + rows, width), jnp.int16)

    swap = [(a, a ^ 1) for a in range(2 * ny)]

    def turn(by):
        return [(a, ((a // 2 + by) % ny) * 2 + a % 2) for a in range(2 * ny)]

    lists, lens, load, operand_near, own_near = call(
        functools.partial(sort_live, ny),
        [slot_columns.T, live_counts, operand_panel, slot_blocks],
        [
            i32((slots * shards * here,)),
            i32((slots * shards,)),
            i32((SLAB_DEV * shards,)),
            jax.ShapeDtypeStruct(operand_panel.shape, operand_panel.dtype),
            jax.ShapeDtypeStruct(slot_blocks.shape, slot_blocks.dtype),
        ],
        [SMEM] * 3 + [VMEM] * 2,
        [pltpu.SemaphoreType.DMA((2,))],
        few=2,
        space=pl.BlockSpec(memory_space=pltpu.HBM),
    )
    turned = [lax.ppermute(slot_blocks, "row", turn(by)) for by in range(1, ny)]
    turned, lists = lax.optimization_barrier((turned, lists))
    blocks = [own_near, lax.ppermute(slot_blocks, "row", swap)]
    blocks += [x for came in turned for x in (came, lax.ppermute(came, "row", swap))]
    ins = [lists, lens, load, operand_near, *blocks]
    scratch = [pltpu.VMEM((depth, width), jnp.bfloat16)]
    flops = 4 * rows * depth * width

    def first(z):
        return jnp.where(lax.rem(z, 2) == 0, 3, 0)

    def second(z):
        return jnp.where(z < 2, 2, 1)

    def third(z):
        return jnp.where(z == 0, 1, jnp.where(z == 1, 3, jnp.where(z == 2, 0, 2)))

    send_a, send_b = call(
        functools.partial(coded_products, (first, second), len(blocks)), ins, [coded] * 2, [VMEM] * 2, scratch, flops, 3
    )
    came_b = lax.ppermute(send_b, "col", [(1, 2), (2, 1)])
    came_a = lax.ppermute(send_a, "col", [(0, 1), (1, 0), (2, 3), (3, 2)])
    passed, own, passed_load, own_load = call(
        functools.partial(plain_products, (third, lambda z: z), len(blocks)),
        ins,
        [f32((rows, width)), f32((rows, width)), i32((8, width)), i32((8, width))],
        [VMEM] * 4,
        scratch,
        flops,
        3,
    )
    send_f, passed = lax.optimization_barrier((send_b, passed))
    came_f = lax.ppermute(send_f, "col", [(0, 2), (3, 1)])
    [send_t] = call(relay, [passed, passed_load, came_a], [coded], [VMEM])
    came_t = lax.ppermute(send_t, "col", [(0, 1), (1, 3), (3, 2), (2, 0)])
    own, own_load = call(
        settle, [own, own_load, came_a, came_b, came_f], [f32((rows, width)), i32((8, width))], [VMEM] * 2
    )
    inflated, totals, load = call(
        inflate, [own, own_load, came_t], [f32((rows, width)), f32((8, width)), i32((SLAB_DEV,))], [VMEM, VMEM, SMEM]
    )
    others = [totals]
    for by in range(ny):
        for flip in (0, 1):
            if by or flip:
                pairs = [(a, ((a // 2 + by) % ny) * 2 + (a % 2 ^ flip)) for a in range(2 * ny)]
                others.append(lax.ppermute(totals, "row", pairs))
    all_rows = rows * lax.axis_size("row")
    [mcl_columns] = call(functools.partial(scale, all_rows), [inflated, *others], [f32((rows, width))], [VMEM])
    return mcl_columns, load


def densify(blocks, columns, counts, first_row, slab_width):
    rows_here, slots = columns.shape
    side = blocks.shape[2]
    places = jnp.arange(slots, dtype=jnp.int32)
    rows_index = first_row + jnp.arange(rows_here, dtype=jnp.int32)
    live = jnp.mod(places[None, :] - rows_index[:, None], slots) < counts[:, None]
    onehot = (columns[:, :, None] == jnp.arange(slab_width, dtype=jnp.int32)[None, None, :]) & live[:, :, None]
    dense = jnp.einsum(
        "kej,kebc->kbjc", onehot.astype(jnp.bfloat16), blocks, preferred_element_type=jnp.float32
    )
    dense = dense.astype(jnp.bfloat16).reshape(rows_here * side, slab_width * side)
    return (dense, jnp.sum(onehot.astype(jnp.float32), axis=(0, 1)))


def body_any(operand_panel, slot_blocks, slot_columns, live_counts):
    gathered = lax.all_gather(slot_blocks, "row", axis=1, tiled=True)
    slab_width = SLAB_DEV * lax.axis_size("col")
    first_row = lax.axis_index("col") * slot_columns.shape[0]
    dense, load = densify(gathered, slot_columns, live_counts, first_row, slab_width)
    partial_terms = jnp.dot(operand_panel, dense, preferred_element_type=jnp.float32)
    expanded, load_mine = (
        lax.psum_scatter(partial_terms, "col", scatter_dimension=1, tiled=True),
        lax.psum_scatter(load, "col", scatter_dimension=0, tiled=True),
    )
    inflated = expanded * expanded
    totals = lax.psum(jnp.sum(inflated, axis=0), "row")
    all_rows = expanded.shape[0] * lax.axis_size("row")
    mcl_columns = inflated / (totals / all_rows + 1e-06)
    return (mcl_columns, load_mine.astype(jnp.int32))


def solution(mesh):
    placed = (
        P(("groups", "row"), "col"),
        P(("groups", "col"), "row", None, None),
        P(("groups", "col"), None),
        P(("groups", "col")),
    )
    return jax.shard_map(
        body_line if mesh.shape["col"] == 4 else body_any,
        mesh=mesh,
        in_specs=placed,
        out_specs=(P(("groups", "row"), "col"), P(("groups", "col"))),
        check_vma=False,
    )
```

```python
import functools

import jax
import jax.numpy as jnp
from jax import lax
from jax.experimental import pallas as pl
from jax.experimental.pallas import tpu as pltpu
from jax.sharding import PartitionSpec as P

SLAB_DEV = 4
SIDE = 128
HEAD = 16
TILE = 256
STEPS = 32700.0
NEAREST = 12582912.0
OCTAVE = 128.0

VMEM = pl.BlockSpec(memory_space=pltpu.VMEM)
SMEM = pl.BlockSpec(memory_space=pltpu.SMEM)


def code_scale(values):
    most = jnp.max(jnp.abs(values), axis=0, keepdims=True)
    octaves = jnp.log2(jnp.maximum(most, 1e-30))
    return jnp.ceil(octaves * OCTAVE)


def encode(values, code):
    scaled = values * (STEPS * jnp.exp2(code * (-1.0 / OCTAVE)))
    return ((scaled + NEAREST) - NEAREST).astype(jnp.int32).astype(jnp.int16)


def head_rows(code, counts):
    shape = (HEAD, code.shape[1])
    row = lax.broadcasted_iota(jnp.int32, shape, 0)
    code = jnp.broadcast_to(code.astype(jnp.int32), shape)
    counts = jnp.broadcast_to(counts, shape)
    return jnp.where(row == 0, code, jnp.where(row == 1, counts, 0)).astype(jnp.int16)


def put_coded(out, lanes, values, counts):
    code = code_scale(values)
    out[pl.ds(0, HEAD), lanes] = head_rows(code, counts)
    out[pl.ds(HEAD, values.shape[0]), lanes] = encode(values, code)


def decode(ref, lanes):
    rows = ref.shape[0] - HEAD
    head = ref[pl.ds(0, HEAD), lanes].astype(jnp.int32).astype(jnp.float32)
    scale = jnp.exp2(head[0:1] * (1.0 / OCTAVE)) * (1.0 / STEPS)
    return ref[pl.ds(HEAD, rows), lanes].astype(jnp.int32).astype(jnp.float32) * scale


def head_counts(ref, lanes):
    return ref[pl.ds(0, HEAD), lanes].astype(jnp.int32)[1:2]


def slot_of(place, ny):
    me = lax.axis_index("row")
    y, core = lax.div(me, 2), lax.rem(me, 2)
    return lax.rem(y + ny - place // 2, ny) * 2 + (core if place % 2 == 0 else 1 - core)


def is_live(columns, counts, k, e):
    slots, rows = columns.shape
    row_index = lax.axis_index("col") * rows + k
    all_rows = rows * lax.axis_size("col")
    return lax.rem(e - row_index + all_rows * slots, slots) < counts[k]


class Plan:
    def __init__(self, ref, rows, slots, shards):
        self.ref, self.rows, self.slots, self.shards = ref, rows, slots, shards
        self.lens = rows * slots * shards
        self.loads = self.lens + slots * shards
        self.size = self.loads + SLAB_DEV * shards

    def entry(self, place, shard, j):
        return (place * self.shards + shard) * self.rows + j

    def length(self, place, shard):
        return self.lens + place * self.shards + shard

    def load(self, column):
        return self.loads + column


def plan_of(ref, operand):
    rows = operand.shape[1] // SIDE
    return Plan(ref, rows, lax.axis_size("row"), lax.axis_size("col"))


def begin(ny, which, columns, counts, operand, own, twin, plan_ref, operand_near, own_near, total, sems):
    copies = [
        pltpu.make_async_copy(far, near, sems.at[j])
        for j, (far, near) in enumerate(((operand, operand_near), (own, own_near)))
    ]
    for copy in copies:
        copy.start()
    slots, rows = columns.shape
    plan = plan_of(plan_ref, operand)

    def clear(j, carry):
        plan_ref[plan.lens + j] = 0
        return carry

    lax.fori_loop(0, plan.size - plan.lens, clear, 0)
    for place in range(slots):
        e = slot_of(place, ny)

        def one(k, carry, place=place, e=e):
            @pl.when(is_live(columns, counts, k, e))
            def _():
                column = columns[e, k]
                plan_ref[plan.load(column)] = plan_ref[plan.load(column)] + 1
                shard = lax.div(column, SLAB_DEV)
                at = plan.length(place, shard)
                length = plan_ref[at]
                plan_ref[plan.entry(place, shard, length)] = k * SLAB_DEV + column - shard * SLAB_DEV
                plan_ref[at] = length + 1

            return carry

        lax.fori_loop(0, rows, one, 0)
    for copy in copies:
        copy.wait()
    total[...] = jnp.zeros_like(total)
    for place, held in enumerate((own_near, twin)):
        add_terms(plan, which(lax.axis_index("col")), place, held, total, operand_near)


def add_terms(plan, shard, place, held, total, operand):
    length = plan.ref[plan.length(place, shard)]

    def term(j):
        entry = jnp.where(j < length, plan.ref[plan.entry(place, shard, jnp.minimum(j, plan.rows - 1))], 0)
        k, column = lax.div(entry, SLAB_DEV), lax.rem(entry, SLAB_DEV)
        block = held[k, 0]
        block = jnp.where(j < length, block, jnp.zeros_like(block))
        left = operand[:, pl.ds(pl.multiple_of(k * SIDE, SIDE), SIDE)]
        lanes = pl.ds(pl.multiple_of(column * SIDE, SIDE), SIDE)
        return lanes, jnp.dot(left, block, preferred_element_type=jnp.float32)

    def step(pair, carry):
        for lanes, value in [term(2 * pair), term(2 * pair + 1)]:
            total[:, lanes] = total[:, lanes] + value
        return carry

    lax.fori_loop(0, lax.div(length + 1, 2), step, 0)


def go_on(which, place, plan_ref, operand, held, _, total):
    add_terms(plan_of(plan_ref, operand), which(lax.axis_index("col")), place, held, total, operand)


def code_sum(which, place, plan_ref, operand, held, total, out):
    plan = plan_of(plan_ref, operand)
    shard = which(lax.axis_index("col"))
    add_terms(plan, shard, place, held, total, operand)

    def body(tile, lanes):
        put_coded(out, lanes, total[:, lanes], counts_of(plan, shard, tile))

    tiles(total.shape[1], body)


def fill(slab, plan, shard, blocks):
    slab[...] = jnp.zeros_like(slab)
    for place, held in enumerate(blocks):

        def one(j, carry, place=place, held=held):
            entry = plan.ref[plan.entry(place, shard, j)]
            k, column = lax.div(entry, SLAB_DEV), lax.rem(entry, SLAB_DEV)
            where = (pl.ds(pl.multiple_of(k * SIDE, SIDE), SIDE), pl.ds(pl.multiple_of(column * SIDE, SIDE), SIDE))
            slab[where] = held[k, 0]
            return carry

        lax.fori_loop(0, plan.ref[plan.length(place, shard)], one, 0)


def counts_of(plan, shard, tile):
    lane = lax.broadcasted_iota(jnp.int32, (1, TILE), 1)
    counts = jnp.zeros((1, TILE), jnp.int32)
    for j in range(TILE // SIDE):
        block = shard * SLAB_DEV + tile * (TILE // SIDE) + j
        counts = jnp.where((lane >= j * SIDE) & (lane < (j + 1) * SIDE), plan.ref[plan.load(block)], counts)
    return counts


def tiles(width, body):
    def step(tile, carry):
        body(tile, pl.ds(pl.multiple_of(tile * TILE, TILE), TILE))
        return carry

    lax.fori_loop(0, width // TILE, step, 0)


def products(coded, plain, nblocks, *refs):
    plan_ref, operand, *blocks = refs[: 2 + nblocks]
    out_coded, *outs, slab = refs[2 + nblocks :]
    plan = plan_of(plan_ref, operand)
    outs, loads = outs[: len(plain)], outs[len(plain) :]

    def one_shard(which, put):
        shard = which(lax.axis_index("col"))
        fill(slab, plan, shard, blocks)

        def body(tile, lanes):
            values = jnp.dot(operand[...], slab[:, lanes], preferred_element_type=jnp.float32)
            put(lanes, values, counts_of(plan, shard, tile))

        tiles(slab.shape[1], body)

    one_shard(coded, functools.partial(put_coded, out_coded))
    for which, out, row in zip(plain, outs, loads):

        def put(lanes, values, counts, out=out, row=row):
            out[:, lanes] = values
            row[:, lanes] = jnp.broadcast_to(counts, (8, TILE))

        one_shard(which, put)


def relay(own, own_load, came, out):
    place = lax.axis_index("col")
    inner = (place == 1) | (place == 2)

    def body(tile, lanes):
        @pl.when(inner)
        def _():
            put_coded(out, lanes, own[:, lanes] + decode(came, lanes), own_load[0:1, lanes] + head_counts(came, lanes))

        @pl.when(jnp.logical_not(inner))
        def _():
            put_coded(out, lanes, own[:, lanes], own_load[0:1, lanes])

    tiles(own.shape[1], body)


def settle(own, own_load, came_b, came_f, out, out_load):
    place = lax.axis_index("col")
    inner = (place == 1) | (place == 2)

    def body(tile, lanes):
        out[:, lanes] = own[:, lanes] + decode(came_f, lanes)
        out_load[:, lanes] = own_load[:, lanes] + head_counts(came_f, lanes)

        @pl.when(inner)
        def _():
            out[:, lanes] = out[:, lanes] + decode(came_b, lanes)
            out_load[:, lanes] = out_load[:, lanes] + head_counts(came_b, lanes)

    tiles(own.shape[1], body)


def inflate(own, own_load, came, out, totals, load):
    def body(tile, lanes):
        expanded = own[:, lanes] + decode(came, lanes)
        inflated = expanded * expanded
        out[:, lanes] = inflated
        totals[:, lanes] = jnp.sum(inflated.reshape(-1, 8, TILE), axis=0)

    tiles(own.shape[1], body)
    for j in range(SLAB_DEV):
        lanes = pl.ds(j * SIDE, SIDE)
        load[j] = jnp.max(own_load[0:1, lanes] + head_counts(came, lanes))


def scale(all_rows, inflated, *refs):
    *totals, out = refs

    def body(tile, lanes):
        total = totals[0][:, lanes]
        for other in totals[1:]:
            total = total + other[:, lanes]
        total = jnp.sum(total, axis=0, keepdims=True)
        out[:, lanes] = inflated[:, lanes] * (1.0 / (total / all_rows + 1e-06))

    tiles(inflated.shape[1], body)


def call(kernel, ins, out_shape, out_specs, scratch=(), flops=0, few=0, far=0, onto=None):
    moved = sum(x.size * x.dtype.itemsize for x in list(ins) + list(out_shape))
    return pl.pallas_call(
        kernel,
        in_specs=[SMEM] * few + [pl.BlockSpec(memory_space=pltpu.HBM)] * far + [VMEM] * (len(ins) - few - far),
        out_shape=out_shape,
        out_specs=out_specs,
        scratch_shapes=list(scratch),
        input_output_aliases=onto or {},
        compiler_params=pltpu.CompilerParams(vmem_limit_bytes=24 << 20),
        cost_estimate=pl.CostEstimate(flops=flops, bytes_accessed=moved, transcendentals=0),
    )(*ins)


def body_line(operand_panel, slot_blocks, slot_columns, live_counts):
    ny = lax.axis_size("row") // 2
    rows, depth = operand_panel.shape
    here, slots = slot_columns.shape
    width = SLAB_DEV * SIDE
    shards = lax.axis_size("col")
    f32 = functools.partial(jax.ShapeDtypeStruct, dtype=jnp.float32)
    i32 = functools.partial(jax.ShapeDtypeStruct, dtype=jnp.int32)
    coded = jax.ShapeDtypeStruct((HEAD + rows, width), jnp.int16)

    swap = [(a, a ^ 1) for a in range(2 * ny)]

    def turn(by):
        return [(a, ((a // 2 + by) % ny) * 2 + a % 2) for a in range(2 * ny)]

    def first(z):
        return 3 - z

    def second(z):
        return jnp.where(z == 0, 2, jnp.where(z == 1, 0, jnp.where(z == 2, 3, 1)))

    def third(z):
        return 3 - second(z)

    flops = 2 * rows * depth * width
    turned = [lax.ppermute(slot_blocks, "row", turn(by)) for by in range(1, ny)]
    twin = lax.ppermute(slot_blocks, "row", swap)
    plan, operand_near, own_near, total = call(
        functools.partial(begin, ny, first),
        [slot_columns.T, live_counts, operand_panel, slot_blocks, twin],
        [
            i32((Plan(None, here, slots, shards).size,)),
            jax.ShapeDtypeStruct(operand_panel.shape, operand_panel.dtype),
            jax.ShapeDtypeStruct(slot_blocks.shape, slot_blocks.dtype),
            f32((rows, width)),
        ],
        [SMEM] + [VMEM] * 3,
        [pltpu.SemaphoreType.DMA((2,))],
        flops // 4,
        few=2,
        far=2,
    )
    turned, plan = lax.optimization_barrier((turned, plan))
    blocks = [own_near, twin]
    blocks += [x for came in turned for x in (came, lax.ppermute(came, "row", swap))]
    for place in range(2, slots - 1):
        [total] = call(
            functools.partial(go_on, first, place),
            [plan, operand_near, blocks[place], total],
            [f32((rows, width))],
            [VMEM],
            (),
            flops // 8,
            1,
            onto={3: 0},
        )
    [send_a] = call(
        functools.partial(code_sum, first, slots - 1),
        [plan, operand_near, blocks[-1], total],
        [coded],
        [VMEM],
        (),
        flops // 8,
        1,
    )
    came_a = lax.ppermute(send_a, "col", [(0, 1), (1, 0), (2, 3), (3, 2)])
    came_b = lax.ppermute(
        send_a,
        ("row", "col"),
        [(4 * r + c, 4 * r + 3 - c if c in (1, 2) else 4 * (r ^ 1) + c) for r in range(2 * ny) for c in range(4)],
    )
    send_f, passed, own, passed_load, own_load = call(
        functools.partial(products, second, (third, lambda z: z), len(blocks)),
        [plan, operand_near, *blocks],
        [coded, f32((rows, width)), f32((rows, width)), i32((8, width)), i32((8, width))],
        [VMEM] * 5,
        [pltpu.VMEM((depth, width), jnp.bfloat16)],
        3 * flops,
        1,
    )
    came_f = lax.ppermute(send_f, "col", [(0, 2), (1, 0), (2, 3), (3, 1)])
    [send_t] = call(relay, [passed, passed_load, came_a], [coded], [VMEM])
    came_t = lax.ppermute(send_t, "col", [(0, 1), (1, 3), (3, 2), (2, 0)])
    own, own_load = call(
        settle, [own, own_load, came_b, came_f], [f32((rows, width)), i32((8, width))], [VMEM] * 2
    )
    inflated, totals, load = call(
        inflate, [own, own_load, came_t], [f32((rows, width)), f32((8, width)), i32((SLAB_DEV,))], [VMEM, VMEM, SMEM]
    )
    others = [totals]
    for by in range(ny):
        for flip in (0, 1):
            if by or flip:
                pairs = [(a, ((a // 2 + by) % ny) * 2 + (a % 2 ^ flip)) for a in range(2 * ny)]
                others.append(lax.ppermute(totals, "row", pairs))
    all_rows = rows * lax.axis_size("row")
    [mcl_columns] = call(functools.partial(scale, all_rows), [inflated, *others], [f32((rows, width))], [VMEM])
    return mcl_columns, load


def densify(blocks, columns, counts, first_row, slab_width):
    rows_here, slots = columns.shape
    side = blocks.shape[2]
    places = jnp.arange(slots, dtype=jnp.int32)
    rows_index = first_row + jnp.arange(rows_here, dtype=jnp.int32)
    live = jnp.mod(places[None, :] - rows_index[:, None], slots) < counts[:, None]
    onehot = (columns[:, :, None] == jnp.arange(slab_width, dtype=jnp.int32)[None, None, :]) & live[:, :, None]
    dense = jnp.einsum(
        "kej,kebc->kbjc", onehot.astype(jnp.bfloat16), blocks, preferred_element_type=jnp.float32
    )
    dense = dense.astype(jnp.bfloat16).reshape(rows_here * side, slab_width * side)
    return (dense, jnp.sum(onehot.astype(jnp.float32), axis=(0, 1)))


def body_any(operand_panel, slot_blocks, slot_columns, live_counts):
    gathered = lax.all_gather(slot_blocks, "row", axis=1, tiled=True)
    slab_width = SLAB_DEV * lax.axis_size("col")
    first_row = lax.axis_index("col") * slot_columns.shape[0]
    dense, load = densify(gathered, slot_columns, live_counts, first_row, slab_width)
    partial_terms = jnp.dot(operand_panel, dense, preferred_element_type=jnp.float32)
    expanded, load_mine = (
        lax.psum_scatter(partial_terms, "col", scatter_dimension=1, tiled=True),
        lax.psum_scatter(load, "col", scatter_dimension=0, tiled=True),
    )
    inflated = expanded * expanded
    totals = lax.psum(jnp.sum(inflated, axis=0), "row")
    all_rows = expanded.shape[0] * lax.axis_size("row")
    mcl_columns = inflated / (totals / all_rows + 1e-06)
    return (mcl_columns, load_mine.astype(jnp.int32))


def solution(mesh):
    placed = (
        P(("groups", "row"), "col"),
        P(("groups", "col"), "row", None, None),
        P(("groups", "col"), None),
        P(("groups", "col")),
    )
    return jax.shard_map(
        body_line if mesh.shape["col"] == 4 else body_any,
        mesh=mesh,
        in_specs=placed,
        out_specs=(P(("groups", "row"), "col"), P(("groups", "col"))),
        check_vma=False,
    )
```

```python
import functools

import jax
import jax.numpy as jnp
from jax import lax
from jax.experimental import pallas as pl
from jax.experimental.pallas import tpu as pltpu
from jax.sharding import PartitionSpec as P

SLAB_DEV = 4
SIDE = 128
HEAD = 16
TILE = 256
ABREAST = 4
PARTS = 2
COST = 1
STEPS = 32700.0
NEAREST = 12582912.0
OCTAVE = 128.0

VMEM = pl.BlockSpec(memory_space=pltpu.VMEM)
SMEM = pl.BlockSpec(memory_space=pltpu.SMEM)


def code_scale(values):
    most = jnp.max(jnp.abs(values), axis=0, keepdims=True)
    octaves = jnp.log2(jnp.maximum(most, 1e-30))
    return jnp.ceil(octaves * OCTAVE)


def encode(values, code):
    scaled = values * (STEPS * jnp.exp2(code * (-1.0 / OCTAVE)))
    return ((scaled + NEAREST) - NEAREST).astype(jnp.int32).astype(jnp.int16)


def head_rows(code, *counts):
    shape = (HEAD, code.shape[1])
    row = lax.broadcasted_iota(jnp.int32, shape, 0)
    head = jnp.broadcast_to(code.astype(jnp.int32), shape)
    for j, one in enumerate(counts):
        head = jnp.where(row > j, jnp.broadcast_to(one, shape), head)
    return head.astype(jnp.int16)


def put_coded(out, lanes, values, *counts):
    code = code_scale(values)
    out[pl.ds(0, HEAD), lanes] = head_rows(code, *counts)
    out[pl.ds(HEAD, values.shape[0]), lanes] = encode(values, code)


def decode(ref, lanes):
    rows = ref.shape[0] - HEAD
    head = ref[pl.ds(0, HEAD), lanes].astype(jnp.int32).astype(jnp.float32)
    scale = jnp.exp2(head[0:1] * (1.0 / OCTAVE)) * (1.0 / STEPS)
    return ref[pl.ds(HEAD, rows), lanes].astype(jnp.int32).astype(jnp.float32) * scale


def head_counts(ref, lanes, part=0):
    return ref[pl.ds(0, HEAD), lanes].astype(jnp.int32)[1 + part : 2 + part]


def slot_of(place, ny):
    me = lax.axis_index("row")
    y, core = lax.div(me, 2), lax.rem(me, 2)
    return lax.rem(y + ny - place // 2, ny) * 2 + (core if place % 2 == 0 else 1 - core)


def is_live(columns, counts, k, e):
    slots, rows = columns.shape
    row_index = lax.axis_index("col") * rows + k
    all_rows = rows * lax.axis_size("col")
    return lax.rem(e - row_index + all_rows * slots, slots) < counts[k]


class Plan:
    def __init__(self, ref, rows, slots, shards):
        self.ref, self.rows, self.slots, self.shards = ref, rows, slots, shards
        self.lens = rows * slots * shards
        self.loads = self.lens + slots * shards
        self.size = self.loads + SLAB_DEV * shards

    def entry(self, place, shard, j):
        return (place * self.shards + shard) * self.rows + j

    def length(self, place, shard):
        return self.lens + place * self.shards + shard

    def load(self, column):
        return self.loads + column


def plan_of(ref, operand):
    rows = operand.shape[1] // SIDE
    return Plan(ref, rows, lax.axis_size("row"), lax.axis_size("col"))


def begin(ny, which, columns, counts, operand, own, twin, plan_ref, operand_near, own_near, total, sems):
    copies = [
        pltpu.make_async_copy(far, near, sems.at[j])
        for j, (far, near) in enumerate(((operand, operand_near), (own, own_near)))
    ]
    for copy in copies:
        copy.start()
    slots, rows = columns.shape
    plan = plan_of(plan_ref, operand)

    def clear(j, carry):
        plan_ref[plan.lens + j] = 0
        return carry

    lax.fori_loop(0, plan.size - plan.lens, clear, 0)
    for place in range(slots):
        e = slot_of(place, ny)

        def one(k, carry, place=place, e=e):
            @pl.when(is_live(columns, counts, k, e))
            def _():
                column = columns[e, k]
                plan_ref[plan.load(column)] = plan_ref[plan.load(column)] + 1
                shard = lax.div(column, SLAB_DEV)
                at = plan.length(place, shard)
                length = plan_ref[at]
                plan_ref[plan.entry(place, shard, length)] = k * SLAB_DEV + column - shard * SLAB_DEV
                plan_ref[at] = length + 1

            return carry

        lax.fori_loop(0, rows, one, 0)
    for copy in copies:
        copy.wait()
    total[...] = jnp.zeros_like(total)
    for place, held in enumerate((own_near, twin)):
        add_terms(plan, which(lax.axis_index("col")), place, held, total, operand_near)


def add_terms(plan, shard, place, held, total, operand):
    length = plan.ref[plan.length(place, shard)]

    def term(j):
        entry = jnp.where(j < length, plan.ref[plan.entry(place, shard, jnp.minimum(j, plan.rows - 1))], 0)
        k, column = lax.div(entry, SLAB_DEV), lax.rem(entry, SLAB_DEV)
        block = held[k, 0]
        block = jnp.where(j < length, block, jnp.zeros_like(block))
        left = operand[:, pl.ds(pl.multiple_of(k * SIDE, SIDE), SIDE)]
        lanes = pl.ds(pl.multiple_of(column * SIDE, SIDE), SIDE)
        return lanes, jnp.dot(left, block, preferred_element_type=jnp.float32)

    def step(some, carry):
        for lanes, value in [term(ABREAST * some + j) for j in range(ABREAST)]:
            total[:, lanes] = total[:, lanes] + value
        return carry

    lax.fori_loop(0, lax.div(length + ABREAST - 1, ABREAST), step, 0)


def go_on(which, place, plan_ref, operand, held, _, total):
    add_terms(plan_of(plan_ref, operand), which(lax.axis_index("col")), place, held, total, operand)


def code_sum(which, place, plan_ref, operand, held, total, out):
    plan = plan_of(plan_ref, operand)
    shard = which(lax.axis_index("col"))
    add_terms(plan, shard, place, held, total, operand)

    def body(tile, lanes):
        put_coded(out, lanes, total[:, lanes], counts_of(plan, shard, tile))

    tiles(total.shape[1], body)


def fill(slab, plan, shard, blocks):
    slab[...] = jnp.zeros_like(slab)
    for place, held in enumerate(blocks):

        def one(j, carry, place=place, held=held):
            entry = plan.ref[plan.entry(place, shard, j)]
            k, column = lax.div(entry, SLAB_DEV), lax.rem(entry, SLAB_DEV)
            where = (pl.ds(pl.multiple_of(k * SIDE, SIDE), SIDE), pl.ds(pl.multiple_of(column * SIDE, SIDE), SIDE))
            slab[where] = held[k, 0]
            return carry

        lax.fori_loop(0, plan.ref[plan.length(place, shard)], one, 0)


def counts_of(plan, shard, tile):
    lane = lax.broadcasted_iota(jnp.int32, (1, TILE), 1)
    counts = jnp.zeros((1, TILE), jnp.int32)
    for j in range(TILE // SIDE):
        block = shard * SLAB_DEV + tile * (TILE // SIDE) + j
        counts = jnp.where((lane >= j * SIDE) & (lane < (j + 1) * SIDE), plan.ref[plan.load(block)], counts)
    return counts


def tiles(width, body):
    def step(tile, carry):
        body(tile, pl.ds(pl.multiple_of(tile * TILE, TILE), TILE))
        return carry

    lax.fori_loop(0, width // TILE, step, 0)


def products(coded, plain, nblocks, *refs):
    plan_ref, operand, *blocks = refs[: 2 + nblocks]
    out_coded, *outs, slab = refs[2 + nblocks :]
    plan = plan_of(plan_ref, operand)
    outs, loads = outs[: len(plain)], outs[len(plain) :]

    def one_shard(which, put):
        shard = which(lax.axis_index("col"))
        fill(slab, plan, shard, blocks)

        def body(tile, lanes):
            values = jnp.dot(operand[...], slab[:, lanes], preferred_element_type=jnp.float32)
            put(lanes, values, counts_of(plan, shard, tile))

        tiles(slab.shape[1], body)

    one_shard(coded, functools.partial(put_coded, out_coded))
    for which, out, row in zip(plain, outs, loads):

        def put(lanes, values, counts, out=out, row=row):
            out[:, lanes] = values
            row[:, lanes] = jnp.broadcast_to(counts, (8, TILE))

        one_shard(which, put)


def relay(own, own_load, came, *outs):
    place = lax.axis_index("col")
    inner = (place == 1) | (place == 2)
    width = outs[0].shape[1]
    for part, out in enumerate(outs):

        def body(tile, lanes, part=part, out=out):
            ats = [pl.ds(pl.multiple_of(j * width + tile * TILE, TILE), TILE) for j in range(len(outs))]
            at = ats[part]

            @pl.when(inner)
            def _():
                counts = [own_load[0:1, one] + head_counts(came, one) for one in ats]
                put_coded(out, lanes, own[:, at] + decode(came, at), *counts)

            @pl.when(jnp.logical_not(inner))
            def _():
                put_coded(out, lanes, own[:, at], *[own_load[0:1, one] for one in ats])

        tiles(width, body)


def settle(own, own_load, came_b, came_f, out, out_load):
    place = lax.axis_index("col")
    inner = (place == 1) | (place == 2)

    def body(tile, lanes):
        out[:, lanes] = own[:, lanes] + decode(came_f, lanes)
        out_load[:, lanes] = own_load[:, lanes] + head_counts(came_f, lanes)

        @pl.when(inner)
        def _():
            out[:, lanes] = out[:, lanes] + decode(came_b, lanes)
            out_load[:, lanes] = out_load[:, lanes] + head_counts(came_b, lanes)

    tiles(own.shape[1], body)


def inflate(part, own, came, out, totals):
    width = out.shape[1]

    def body(tile, lanes):
        at = pl.ds(pl.multiple_of(part * width + tile * TILE, TILE), TILE)
        expanded = own[:, at] + decode(came, lanes)
        inflated = expanded * expanded
        out[:, lanes] = inflated
        totals[:, lanes] = jnp.sum(inflated.reshape(-1, 8, TILE), axis=0)

    tiles(width, body)


def count(own_load, came, load):
    width = came.shape[1]
    for j in range(SLAB_DEV):
        lanes, at = pl.ds(j * SIDE % width, SIDE), pl.ds(j * SIDE, SIDE)
        load[j] = jnp.max(own_load[0:1, at] + head_counts(came, lanes, j * SIDE // width))


def scale(all_rows, part, inflated, *refs):
    *totals, out, scaled, sems = refs[:-4] + refs[-3:] if part else refs
    rows, width = inflated.shape
    total = totals[0][...]
    for other in totals[1:]:
        total = total + other[...]
    total = jnp.sum(total, axis=0, keepdims=True)
    factor = 1.0 / (total / all_rows + 1e-06)
    few = rows // sems.shape[0]
    copies = []
    for j in range(sems.shape[0]):
        these = pl.ds(j * few, few)
        scaled[these, :] = inflated[these, :] * factor
        copy = pltpu.make_async_copy(scaled.at[these, :], out.at[these, pl.ds(part * width, width)], sems.at[j])
        copy.start()
        copies.append(copy)
    for copy in copies:
        copy.wait()


def call(kernel, ins, out_shape, out_specs, scratch=(), flops=0, few=0, far=0, onto=None, last=False):
    moved = sum(x.size * x.dtype.itemsize for x in list(ins) + list(out_shape))
    return pl.pallas_call(
        kernel,
        in_specs=[SMEM] * few + [pl.BlockSpec(memory_space=pltpu.HBM)] * far + [VMEM] * (len(ins) - few - far - last) + [pl.BlockSpec(memory_space=pl.ANY)] * last,
        out_shape=out_shape,
        out_specs=out_specs,
        scratch_shapes=list(scratch),
        input_output_aliases=onto or {},
        compiler_params=pltpu.CompilerParams(vmem_limit_bytes=24 << 20),
        cost_estimate=pl.CostEstimate(flops=flops // COST, bytes_accessed=moved // COST, transcendentals=0),
    )(*ins)


def body_line(operand_panel, slot_blocks, slot_columns, live_counts):
    ny = lax.axis_size("row") // 2
    rows, depth = operand_panel.shape
    here, slots = slot_columns.shape
    width = SLAB_DEV * SIDE
    shards = lax.axis_size("col")
    f32 = functools.partial(jax.ShapeDtypeStruct, dtype=jnp.float32)
    i32 = functools.partial(jax.ShapeDtypeStruct, dtype=jnp.int32)
    coded = jax.ShapeDtypeStruct((HEAD + rows, width), jnp.int16)

    swap = [(a, a ^ 1) for a in range(2 * ny)]

    def turn(by):
        return [(a, ((a // 2 + by) % ny) * 2 + a % 2) for a in range(2 * ny)]

    def first(z):
        return 3 - z

    def second(z):
        return jnp.where(z == 0, 2, jnp.where(z == 1, 0, jnp.where(z == 2, 3, 1)))

    def third(z):
        return 3 - second(z)

    flops = 2 * rows * depth * width
    turned = [lax.ppermute(slot_blocks, "row", turn(by)) for by in range(1, ny)]
    twin = lax.ppermute(slot_blocks, "row", swap)
    plan, operand_near, own_near, total = call(
        functools.partial(begin, ny, first),
        [slot_columns.T, live_counts, operand_panel, slot_blocks, twin],
        [
            i32((Plan(None, here, slots, shards).size,)),
            jax.ShapeDtypeStruct(operand_panel.shape, operand_panel.dtype),
            jax.ShapeDtypeStruct(slot_blocks.shape, slot_blocks.dtype),
            f32((rows, width)),
        ],
        [SMEM] + [VMEM] * 3,
        [pltpu.SemaphoreType.DMA((2,))],
        flops // 4,
        few=2,
        far=2,
    )
    turned, plan = lax.optimization_barrier((turned, plan))
    blocks = [own_near, twin]
    blocks += [x for came in turned for x in (came, lax.ppermute(came, "row", swap))]
    for place in range(2, slots - 1):
        [total] = call(
            functools.partial(go_on, first, place),
            [plan, operand_near, blocks[place], total],
            [f32((rows, width))],
            [VMEM],
            (),
            flops // 8,
            1,
            onto={3: 0},
        )
    [send_a] = call(
        functools.partial(code_sum, first, slots - 1),
        [plan, operand_near, blocks[-1], total],
        [coded],
        [VMEM],
        (),
        flops // 8,
        1,
    )
    came_a = lax.ppermute(send_a, "col", [(0, 1), (1, 0), (2, 3), (3, 2)])
    came_b = lax.ppermute(
        send_a,
        ("row", "col"),
        [(4 * r + c, 4 * r + 3 - c if c in (1, 2) else 4 * (r ^ 1) + c) for r in range(2 * ny) for c in range(4)],
    )
    send_f, passed, own, passed_load, own_load = call(
        functools.partial(products, second, (third, lambda z: z), len(blocks)),
        [plan, operand_near, *blocks],
        [coded, f32((rows, width)), f32((rows, width)), i32((8, width)), i32((8, width))],
        [VMEM] * 5,
        [pltpu.VMEM((depth, width), jnp.bfloat16)],
        3 * flops,
        1,
    )
    came_f = lax.ppermute(send_f, "col", [(0, 2), (1, 0), (2, 3), (3, 1)])
    came_a, came_b = lax.optimization_barrier((came_a, came_b))
    sent = jax.ShapeDtypeStruct((HEAD + rows, width // PARTS), jnp.int16)
    send_t = call(relay, [passed, passed_load, came_a], [sent] * PARTS, [VMEM] * PARTS)
    came_t = [lax.ppermute(one, "col", [(0, 1), (1, 3), (3, 2), (2, 0)]) for one in send_t]
    own, own_load = call(
        settle, [own, own_load, came_b, came_f], [f32((rows, width)), i32((8, width))], [VMEM] * 2
    )
    all_rows = rows * lax.axis_size("row")
    hbm = pl.BlockSpec(memory_space=pl.ANY)
    result = []
    [load] = call(count, [own_load, came_t[0]], [i32((SLAB_DEV,))], [SMEM])
    for part in range(PARTS):
        inflated, totals = call(
            functools.partial(inflate, part),
            [own, came_t[part]],
            [f32((rows, width // PARTS)), f32((8, width // PARTS))],
            [VMEM] * 2,
        )
        others = [totals]
        for by in range(ny):
            for flip in (0, 1):
                if by or flip:
                    pairs = [(a, ((a // 2 + by) % ny) * 2 + (a % 2 ^ flip)) for a in range(2 * ny)]
                    others.append(lax.ppermute(totals, "row", pairs))
        result = call(
            functools.partial(scale, all_rows, part),
            [inflated, *others, *result],
            [f32((rows, width))],
            [hbm],
            [pltpu.VMEM((rows, width // PARTS), jnp.float32), pltpu.SemaphoreType.DMA((4,))],
            onto={1 + len(others): 0} if part else None,
            last=bool(part),
        )
    return result[0], load


def densify(blocks, columns, counts, first_row, slab_width):
    rows_here, slots = columns.shape
    side = blocks.shape[2]
    places = jnp.arange(slots, dtype=jnp.int32)
    rows_index = first_row + jnp.arange(rows_here, dtype=jnp.int32)
    live = jnp.mod(places[None, :] - rows_index[:, None], slots) < counts[:, None]
    onehot = (columns[:, :, None] == jnp.arange(slab_width, dtype=jnp.int32)[None, None, :]) & live[:, :, None]
    dense = jnp.einsum(
        "kej,kebc->kbjc", onehot.astype(jnp.bfloat16), blocks, preferred_element_type=jnp.float32
    )
    dense = dense.astype(jnp.bfloat16).reshape(rows_here * side, slab_width * side)
    return (dense, jnp.sum(onehot.astype(jnp.float32), axis=(0, 1)))


def body_any(operand_panel, slot_blocks, slot_columns, live_counts):
    gathered = lax.all_gather(slot_blocks, "row", axis=1, tiled=True)
    slab_width = SLAB_DEV * lax.axis_size("col")
    first_row = lax.axis_index("col") * slot_columns.shape[0]
    dense, load = densify(gathered, slot_columns, live_counts, first_row, slab_width)
    partial_terms = jnp.dot(operand_panel, dense, preferred_element_type=jnp.float32)
    expanded, load_mine = (
        lax.psum_scatter(partial_terms, "col", scatter_dimension=1, tiled=True),
        lax.psum_scatter(load, "col", scatter_dimension=0, tiled=True),
    )
    inflated = expanded * expanded
    totals = lax.psum(jnp.sum(inflated, axis=0), "row")
    all_rows = expanded.shape[0] * lax.axis_size("row")
    mcl_columns = inflated / (totals / all_rows + 1e-06)
    return (mcl_columns, load_mine.astype(jnp.int32))


def solution(mesh):
    placed = (
        P(("groups", "row"), "col"),
        P(("groups", "col"), "row", None, None),
        P(("groups", "col"), None),
        P(("groups", "col")),
    )
    return jax.shard_map(
        body_line if mesh.shape["col"] == 4 else body_any,
        mesh=mesh,
        in_specs=placed,
        out_specs=(P(("groups", "row"), "col"), P(("groups", "col"))),
        check_vma=False,
    )
```

```python
import functools

import jax
import jax.numpy as jnp
from jax import lax
from jax.experimental import pallas as pl
from jax.experimental.pallas import tpu as pltpu
from jax.sharding import PartitionSpec as P

SLAB_DEV = 4
SIDE = 128
HEAD = 16
TILE = 256
ABREAST = 4
PARTS = 2
COST = 1
STEPS = 32700.0
NEAREST = 12582912.0
OCTAVE = 128.0

ALL = list(range(SLAB_DEV))

VMEM = pl.BlockSpec(memory_space=pltpu.VMEM)
SMEM = pl.BlockSpec(memory_space=pltpu.SMEM)


def blocks_of(part):
    return ALL[part * SLAB_DEV // PARTS : (part + 1) * SLAB_DEV // PARTS]


def code_scale(values):
    most = jnp.max(jnp.abs(values), axis=0, keepdims=True)
    octaves = jnp.log2(jnp.maximum(most, 1e-30))
    return jnp.ceil(octaves * OCTAVE)


def encode(values, code):
    scaled = values * (STEPS * jnp.exp2(code * (-1.0 / OCTAVE)))
    return ((scaled + NEAREST) - NEAREST).astype(jnp.int32).astype(jnp.int16)


def put_coded(outs, values, counts):
    row = lax.broadcasted_iota(jnp.int32, counts.shape, 0)
    heads = [jnp.where(row < SLAB_DEV, 0, counts) for _ in outs]
    for block, get in values:
        value = get()
        rows = value.shape[0]
        code = code_scale(value)
        coded = encode(value, code)
        for j, (out, held) in enumerate(outs):
            if block in held:
                at = held.index(block)
                out[pl.ds(at * rows, rows), :] = coded
                heads[j] = jnp.where(row == at, jnp.broadcast_to(code.astype(jnp.int32), counts.shape), heads[j])
    for (out, _), head in zip(outs, heads):
        out[pl.ds(out.shape[0] - HEAD, HEAD), :] = head.astype(jnp.int16)


def head_of(ref):
    return ref[pl.ds(ref.shape[0] - HEAD, HEAD), :].astype(jnp.int32)


def decode(ref, head, at, rows):
    scale = jnp.exp2(head[at : at + 1].astype(jnp.float32) * (1.0 / OCTAVE)) * (1.0 / STEPS)
    return ref[pl.ds(at * rows, rows), :].astype(jnp.int32).astype(jnp.float32) * scale


def lanes_of(block):
    return pl.ds(block * SIDE, SIDE)


def slot_of(place, ny):
    me = lax.axis_index("row")
    y, core = lax.div(me, 2), lax.rem(me, 2)
    return lax.rem(y + ny - place // 2, ny) * 2 + (core if place % 2 == 0 else 1 - core)


def is_live(columns, counts, k, e):
    slots, rows = columns.shape
    row_index = lax.axis_index("col") * rows + k
    all_rows = rows * lax.axis_size("col")
    return lax.rem(e - row_index + all_rows * slots, slots) < counts[k]


class Plan:
    def __init__(self, ref, rows, slots, shards):
        self.ref, self.rows, self.slots, self.shards = ref, rows, slots, shards
        self.lens = rows * slots * shards
        self.loads = self.lens + slots * shards
        self.size = self.loads + SLAB_DEV * shards

    def entry(self, place, shard, j):
        return (place * self.shards + shard) * self.rows + j

    def length(self, place, shard):
        return self.lens + place * self.shards + shard

    def load(self, column):
        return self.loads + column


def plan_of(ref, operand):
    rows = operand.shape[1] // SIDE
    return Plan(ref, rows, lax.axis_size("row"), lax.axis_size("col"))


def begin(ny, which, columns, counts, operand, own, twin, plan_ref, operand_near, own_near, total, sems):
    copies = [
        pltpu.make_async_copy(far, near, sems.at[j])
        for j, (far, near) in enumerate(((operand, operand_near), (own, own_near)))
    ]
    for copy in copies:
        copy.start()
    slots, rows = columns.shape
    plan = plan_of(plan_ref, operand)

    def clear(j, carry):
        plan_ref[plan.lens + j] = 0
        return carry

    lax.fori_loop(0, plan.size - plan.lens, clear, 0)
    for place in range(slots):
        e = slot_of(place, ny)

        def one(k, carry, place=place, e=e):
            @pl.when(is_live(columns, counts, k, e))
            def _():
                column = columns[e, k]
                plan_ref[plan.load(column)] = plan_ref[plan.load(column)] + 1
                shard = lax.div(column, SLAB_DEV)
                at = plan.length(place, shard)
                length = plan_ref[at]
                plan_ref[plan.entry(place, shard, length)] = k * SLAB_DEV + column - shard * SLAB_DEV
                plan_ref[at] = length + 1

            return carry

        lax.fori_loop(0, rows, one, 0)
    for copy in copies:
        copy.wait()
    total[...] = jnp.zeros_like(total)
    for place, held in enumerate((own_near, twin)):
        add_terms(plan, which(lax.axis_index("col")), place, held, total, operand_near)


def add_terms(plan, shard, place, held, total, operand):
    length = plan.ref[plan.length(place, shard)]

    def term(j):
        entry = jnp.where(j < length, plan.ref[plan.entry(place, shard, jnp.minimum(j, plan.rows - 1))], 0)
        k, column = lax.div(entry, SLAB_DEV), lax.rem(entry, SLAB_DEV)
        block = held[k, 0]
        block = jnp.where(j < length, block, jnp.zeros_like(block))
        left = operand[:, pl.ds(pl.multiple_of(k * SIDE, SIDE), SIDE)]
        lanes = pl.ds(pl.multiple_of(column * SIDE, SIDE), SIDE)
        return lanes, jnp.dot(left, block, preferred_element_type=jnp.float32)

    def step(some, carry):
        for lanes, value in [term(ABREAST * some + j) for j in range(ABREAST)]:
            total[:, lanes] = total[:, lanes] + value
        return carry

    lax.fori_loop(0, lax.div(length + ABREAST - 1, ABREAST), step, 0)


def go_on(which, place, plan_ref, operand, held, _, total):
    add_terms(plan_of(plan_ref, operand), which(lax.axis_index("col")), place, held, total, operand)


def code_sum(which, place, plan_ref, operand, held, total, out):
    plan = plan_of(plan_ref, operand)
    shard = which(lax.axis_index("col"))
    add_terms(plan, shard, place, held, total, operand)
    values = [(b, lambda b=b: total[:, lanes_of(b)]) for b in range(SLAB_DEV)]
    put_coded([(out, ALL)], values, counts_of(plan, shard))


def fill(slab, plan, shard, blocks):
    slab[...] = jnp.zeros_like(slab)
    for place, held in enumerate(blocks):

        def one(j, carry, place=place, held=held):
            entry = plan.ref[plan.entry(place, shard, j)]
            k, column = lax.div(entry, SLAB_DEV), lax.rem(entry, SLAB_DEV)
            where = (pl.ds(pl.multiple_of(k * SIDE, SIDE), SIDE), pl.ds(pl.multiple_of(column * SIDE, SIDE), SIDE))
            slab[where] = held[k, 0]
            return carry

        lax.fori_loop(0, plan.ref[plan.length(place, shard)], one, 0)


def counts_of(plan, shard):
    row = lax.broadcasted_iota(jnp.int32, (HEAD, SIDE), 0)
    head = jnp.zeros((HEAD, SIDE), jnp.int32)
    for b in range(SLAB_DEV):
        head = jnp.where(row == SLAB_DEV + b, plan.ref[plan.load(shard * SLAB_DEV + b)], head)
    return head


def tiles(width, body):
    def step(tile, carry):
        body(tile, pl.ds(pl.multiple_of(tile * TILE, TILE), TILE))
        return carry

    lax.fori_loop(0, width // TILE, step, 0)


def coded_product(which, nblocks, plan_ref, operand, *refs):
    blocks, (whole, *parts, slab) = refs[:nblocks], refs[nblocks:]
    plan = plan_of(plan_ref, operand)
    shard = which(lax.axis_index("col"))
    fill(slab, plan, shard, blocks)
    done = {}

    def values(block):
        tile, at = block * SIDE // TILE, block * SIDE % TILE
        if tile not in done:
            lanes = pl.ds(tile * TILE, TILE)
            done[tile] = jnp.dot(operand[...], slab[:, lanes], preferred_element_type=jnp.float32)
        return done[tile][:, at : at + SIDE]

    outs = [(whole, ALL)] + [(part, blocks_of(j)) for j, part in enumerate(parts)]
    put_coded(outs, [(b, functools.partial(values, b)) for b in ALL], counts_of(plan, shard))


def plain_products(plain, nblocks, plan_ref, operand, *refs):
    blocks, (*outs, slab) = refs[:nblocks], refs[nblocks:]
    outs, loads = outs[: len(plain)], outs[len(plain) :]
    plan = plan_of(plan_ref, operand)
    for which, out, row in zip(plain, outs, loads):
        shard = which(lax.axis_index("col"))
        fill(slab, plan, shard, blocks)

        def body(tile, lanes, out=out):
            out[:, lanes] = jnp.dot(operand[...], slab[:, lanes], preferred_element_type=jnp.float32)

        tiles(slab.shape[1], body)
        row[...] = counts_of(plan, shard)


def relay(part, own, own_load, came, out):
    place = lax.axis_index("col")
    inner = (place == 1) | (place == 2)
    held, rows = blocks_of(part), own.shape[0]

    @pl.when(inner)
    def _():
        head = head_of(came)
        values = [
            (b, lambda at=at, b=b: own[:, lanes_of(b)] + decode(came, head, at, rows)) for at, b in enumerate(held)
        ]
        put_coded([(out, held)], values, own_load[...] + head)

    @pl.when(jnp.logical_not(inner))
    def _():
        put_coded([(out, held)], [(b, lambda b=b: own[:, lanes_of(b)]) for b in held], own_load[...])


def settle(own, own_load, came_b, came_f, out, out_load):
    place = lax.axis_index("col")
    inner = (place == 1) | (place == 2)
    rows, head = own.shape[0], head_of(came_f)
    out_load[...] = own_load[...] + head
    for b in ALL:
        out[:, lanes_of(b)] = own[:, lanes_of(b)] + decode(came_f, head, b, rows)

    @pl.when(inner)
    def _():
        head = head_of(came_b)
        out_load[...] = out_load[...] + head
        for b in ALL:
            out[:, lanes_of(b)] = out[:, lanes_of(b)] + decode(came_b, head, b, rows)


def inflate(part, own, came, out, totals):
    rows, head = own.shape[0], head_of(came)
    for at, b in enumerate(blocks_of(part)):
        expanded = own[:, lanes_of(b)] + decode(came, head, at, rows)
        inflated = expanded * expanded
        out[:, lanes_of(at)] = inflated
        totals[:, lanes_of(at)] = jnp.sum(inflated.reshape(-1, 8, SIDE), axis=0)


def count(own_load, came, load):
    head = own_load[...] + head_of(came)
    for j in range(SLAB_DEV):
        load[j] = jnp.max(head[SLAB_DEV + j : SLAB_DEV + j + 1])


def scale(all_rows, part, inflated, *refs):
    *totals, out, scaled, sems = refs[:-4] + refs[-3:] if part else refs
    rows, width = inflated.shape
    total = totals[0][...]
    for other in totals[1:]:
        total = total + other[...]
    total = jnp.sum(total, axis=0, keepdims=True)
    factor = 1.0 / (total / all_rows + 1e-06)
    few = rows // sems.shape[0]
    copies = []
    for j in range(sems.shape[0]):
        these = pl.ds(j * few, few)
        scaled[these, :] = inflated[these, :] * factor
        copy = pltpu.make_async_copy(scaled.at[these, :], out.at[these, pl.ds(part * width, width)], sems.at[j])
        copy.start()
        copies.append(copy)
    for copy in copies:
        copy.wait()


def call(kernel, ins, out_shape, out_specs, scratch=(), flops=0, few=0, far=0, onto=None, last=False):
    moved = sum(x.size * x.dtype.itemsize for x in list(ins) + list(out_shape))
    return pl.pallas_call(
        kernel,
        in_specs=[SMEM] * few + [pl.BlockSpec(memory_space=pltpu.HBM)] * far + [VMEM] * (len(ins) - few - far - last) + [pl.BlockSpec(memory_space=pl.ANY)] * last,
        out_shape=out_shape,
        out_specs=out_specs,
        scratch_shapes=list(scratch),
        input_output_aliases=onto or {},
        compiler_params=pltpu.CompilerParams(vmem_limit_bytes=24 << 20),
        cost_estimate=pl.CostEstimate(flops=flops // COST, bytes_accessed=moved // COST, transcendentals=0),
    )(*ins)


def body_line(operand_panel, slot_blocks, slot_columns, live_counts):
    ny = lax.axis_size("row") // 2
    rows, depth = operand_panel.shape
    here, slots = slot_columns.shape
    width = SLAB_DEV * SIDE
    shards = lax.axis_size("col")
    f32 = functools.partial(jax.ShapeDtypeStruct, dtype=jnp.float32)
    i32 = functools.partial(jax.ShapeDtypeStruct, dtype=jnp.int32)
    coded = jax.ShapeDtypeStruct((SLAB_DEV * rows + HEAD, SIDE), jnp.int16)

    swap = [(a, a ^ 1) for a in range(2 * ny)]

    def turn(by):
        return [(a, ((a // 2 + by) % ny) * 2 + a % 2) for a in range(2 * ny)]

    def first(z):
        return 3 - z

    def second(z):
        return jnp.where(z == 0, 2, jnp.where(z == 1, 0, jnp.where(z == 2, 3, 1)))

    def third(z):
        return 3 - second(z)

    flops = 2 * rows * depth * width
    turned = [lax.ppermute(slot_blocks, "row", turn(by)) for by in range(1, ny)]
    twin = lax.ppermute(slot_blocks, "row", swap)
    plan, operand_near, own_near, total = call(
        functools.partial(begin, ny, second),
        [slot_columns.T, live_counts, operand_panel, slot_blocks, twin],
        [
            i32((Plan(None, here, slots, shards).size,)),
            jax.ShapeDtypeStruct(operand_panel.shape, operand_panel.dtype),
            jax.ShapeDtypeStruct(slot_blocks.shape, slot_blocks.dtype),
            f32((rows, width)),
        ],
        [SMEM] + [VMEM] * 3,
        [pltpu.SemaphoreType.DMA((2,))],
        flops // 4,
        few=2,
        far=2,
    )
    turned, plan = lax.optimization_barrier((turned, plan))
    blocks = [own_near, twin]
    blocks += [x for came in turned for x in (came, lax.ppermute(came, "row", swap))]
    for place in range(2, slots - 1):
        [total] = call(
            functools.partial(go_on, second, place),
            [plan, operand_near, blocks[place], total],
            [f32((rows, width))],
            [VMEM],
            (),
            flops // 8,
            1,
            onto={3: 0},
        )
    [send_f] = call(
        functools.partial(code_sum, second, slots - 1),
        [plan, operand_near, blocks[-1], total],
        [coded],
        [VMEM],
        (),
        flops // 8,
        1,
    )
    came_f = lax.ppermute(send_f, "col", [(0, 2), (1, 0), (2, 3), (3, 1)])
    ins = [plan, operand_near, *blocks]
    slab = [pltpu.VMEM((depth, width), jnp.bfloat16)]
    part_coded = jax.ShapeDtypeStruct((SLAB_DEV // PARTS * rows + HEAD, SIDE), jnp.int16)
    send_b, *send_a = call(
        functools.partial(coded_product, first, len(blocks)),
        ins,
        [coded] + [part_coded] * PARTS,
        [VMEM] * (1 + PARTS),
        slab,
        flops,
        1,
    )
    came_a = [lax.ppermute(one, "col", [(0, 1), (1, 0), (2, 3), (3, 2)]) for one in send_a]
    came_b = lax.ppermute(
        send_b,
        ("row", "col"),
        [(4 * r + c, 4 * r + 3 - c if c in (1, 2) else 4 * (r ^ 1) + c) for r in range(2 * ny) for c in range(4)],
    )
    ins[0], came_f = lax.optimization_barrier((ins[0], came_f))
    passed, own, passed_load, own_load = call(
        functools.partial(plain_products, (third, lambda z: z), len(blocks)),
        ins,
        [f32((rows, width)), f32((rows, width)), i32((HEAD, SIDE)), i32((HEAD, SIDE))],
        [VMEM] * 4,
        slab,
        2 * flops,
        1,
    )
    came_a[-1], came_b = lax.optimization_barrier((came_a[-1], came_b))
    came_t = []
    for part in range(PARTS):
        [send_t] = call(
            functools.partial(relay, part), [passed, passed_load, came_a[part]], [part_coded], [VMEM]
        )
        came_t.append(lax.ppermute(send_t, "col", [(0, 1), (1, 3), (3, 2), (2, 0)]))
    own, own_load = call(
        settle, [own, own_load, came_b, came_f], [f32((rows, width)), i32((HEAD, SIDE))], [VMEM] * 2
    )
    all_rows = rows * lax.axis_size("row")
    hbm = pl.BlockSpec(memory_space=pl.ANY)
    result = []
    [load] = call(count, [own_load, came_t[0]], [i32((SLAB_DEV,))], [SMEM])
    for part in range(PARTS):
        inflated, totals = call(
            functools.partial(inflate, part),
            [own, came_t[part]],
            [f32((rows, width // PARTS)), f32((8, width // PARTS))],
            [VMEM] * 2,
        )
        others = [totals]
        for by in range(ny):
            for flip in (0, 1):
                if by or flip:
                    pairs = [(a, ((a // 2 + by) % ny) * 2 + (a % 2 ^ flip)) for a in range(2 * ny)]
                    others.append(lax.ppermute(totals, "row", pairs))
        result = call(
            functools.partial(scale, all_rows, part),
            [inflated, *others, *result],
            [f32((rows, width))],
            [hbm],
            [pltpu.VMEM((rows, width // PARTS), jnp.float32), pltpu.SemaphoreType.DMA((4,))],
            onto={1 + len(others): 0} if part else None,
            last=bool(part),
        )
    return result[0], load


def densify(blocks, columns, counts, first_row, slab_width):
    rows_here, slots = columns.shape
    side = blocks.shape[2]
    places = jnp.arange(slots, dtype=jnp.int32)
    rows_index = first_row + jnp.arange(rows_here, dtype=jnp.int32)
    live = jnp.mod(places[None, :] - rows_index[:, None], slots) < counts[:, None]
    onehot = (columns[:, :, None] == jnp.arange(slab_width, dtype=jnp.int32)[None, None, :]) & live[:, :, None]
    dense = jnp.einsum(
        "kej,kebc->kbjc", onehot.astype(jnp.bfloat16), blocks, preferred_element_type=jnp.float32
    )
    dense = dense.astype(jnp.bfloat16).reshape(rows_here * side, slab_width * side)
    return (dense, jnp.sum(onehot.astype(jnp.float32), axis=(0, 1)))


def body_any(operand_panel, slot_blocks, slot_columns, live_counts):
    gathered = lax.all_gather(slot_blocks, "row", axis=1, tiled=True)
    slab_width = SLAB_DEV * lax.axis_size("col")
    first_row = lax.axis_index("col") * slot_columns.shape[0]
    dense, load = densify(gathered, slot_columns, live_counts, first_row, slab_width)
    partial_terms = jnp.dot(operand_panel, dense, preferred_element_type=jnp.float32)
    expanded, load_mine = (
        lax.psum_scatter(partial_terms, "col", scatter_dimension=1, tiled=True),
        lax.psum_scatter(load, "col", scatter_dimension=0, tiled=True),
    )
    inflated = expanded * expanded
    totals = lax.psum(jnp.sum(inflated, axis=0), "row")
    all_rows = expanded.shape[0] * lax.axis_size("row")
    mcl_columns = inflated / (totals / all_rows + 1e-06)
    return (mcl_columns, load_mine.astype(jnp.int32))


def solution(mesh):
    placed = (
        P(("groups", "row"), "col"),
        P(("groups", "col"), "row", None, None),
        P(("groups", "col"), None),
        P(("groups", "col")),
    )
    return jax.shard_map(
        body_line if mesh.shape["col"] == 4 else body_any,
        mesh=mesh,
        in_specs=placed,
        out_specs=(P(("groups", "row"), "col"), P(("groups", "col"))),
        check_vma=False,
    )
```

```python
import functools

import jax
import jax.numpy as jnp
from jax import lax
from jax.experimental import pallas as pl
from jax.experimental.pallas import tpu as pltpu
from jax.sharding import PartitionSpec as P

SLAB_DEV = 4
SIDE = 128
HEAD = 16
TILE = 256
ABREAST = 4
PARTS = 2
COST = 1
STEPS = 32700.0
NEAREST = 12582912.0
OCTAVE = 128.0

ALL = list(range(SLAB_DEV))

VMEM = pl.BlockSpec(memory_space=pltpu.VMEM)
SMEM = pl.BlockSpec(memory_space=pltpu.SMEM)


def blocks_of(part):
    return ALL[part * SLAB_DEV // PARTS : (part + 1) * SLAB_DEV // PARTS]


def is_inner():
    place = lax.axis_index("col")
    return (place == 1) | (place == 2)


def code_scale(values):
    most = jnp.max(jnp.abs(values), axis=0, keepdims=True)
    octaves = jnp.log2(jnp.maximum(most, 1e-30))
    return jnp.ceil(octaves * OCTAVE)


def encode(values, code):
    scaled = values * (STEPS * jnp.exp2(code * (-1.0 / OCTAVE)))
    return ((scaled + NEAREST) - NEAREST).astype(jnp.int32).astype(jnp.int16)


def put_coded(outs, values, counts):
    row = lax.broadcasted_iota(jnp.int32, counts.shape, 0)
    heads = [jnp.where(row < SLAB_DEV, 0, counts) for _ in outs]
    for block, get in values:
        value = get()
        rows = value.shape[0]
        code = code_scale(value)
        coded = encode(value, code)
        for j, (out, held) in enumerate(outs):
            if block in held:
                at = held.index(block)
                out[pl.ds(at * rows, rows), :] = coded
                heads[j] = jnp.where(row == at, jnp.broadcast_to(code.astype(jnp.int32), counts.shape), heads[j])
    for (out, _), head in zip(outs, heads):
        out[pl.ds(out.shape[0] - HEAD, HEAD), :] = head.astype(jnp.int16)


def head_of(ref):
    return ref[pl.ds(ref.shape[0] - HEAD, HEAD), :].astype(jnp.int32)


def decode(ref, head, at, rows):
    scale = jnp.exp2(head[at : at + 1].astype(jnp.float32) * (1.0 / OCTAVE)) * (1.0 / STEPS)
    return ref[pl.ds(at * rows, rows), :].astype(jnp.int32).astype(jnp.float32) * scale


def lanes_of(block):
    return pl.ds(block * SIDE, SIDE)


def slot_of(place, ny):
    me = lax.axis_index("row")
    y, core = lax.div(me, 2), lax.rem(me, 2)
    return lax.rem(y + ny - place // 2, ny) * 2 + (core if place % 2 == 0 else 1 - core)


def is_live(columns, counts, k, e):
    slots, rows = columns.shape
    row_index = lax.axis_index("col") * rows + k
    all_rows = rows * lax.axis_size("col")
    return lax.rem(e - row_index + all_rows * slots, slots) < counts[k]


class Plan:
    def __init__(self, ref, rows, slots, shards):
        self.ref, self.rows, self.slots, self.shards = ref, rows, slots, shards
        self.lens = rows * slots * shards
        self.loads = self.lens + slots * shards
        self.size = self.loads + SLAB_DEV * shards

    def entry(self, place, shard, j):
        return (place * self.shards + shard) * self.rows + j

    def length(self, place, shard):
        return self.lens + place * self.shards + shard

    def load(self, column):
        return self.loads + column


def plan_of(ref, operand):
    rows = operand.shape[1] // SIDE
    return Plan(ref, rows, lax.axis_size("row"), lax.axis_size("col"))


def begin(ny, which, columns, counts, operand, own, twin, plan_ref, operand_near, own_near, total, sems):
    copies = [
        pltpu.make_async_copy(far, near, sems.at[j])
        for j, (far, near) in enumerate(((operand, operand_near), (own, own_near)))
    ]
    for copy in copies:
        copy.start()
    slots, rows = columns.shape
    plan = plan_of(plan_ref, operand)

    def clear(j, carry):
        plan_ref[plan.lens + j] = 0
        return carry

    lax.fori_loop(0, plan.size - plan.lens, clear, 0)
    for place in range(slots):
        e = slot_of(place, ny)

        def one(k, carry, place=place, e=e):
            @pl.when(is_live(columns, counts, k, e))
            def _():
                column = columns[e, k]
                plan_ref[plan.load(column)] = plan_ref[plan.load(column)] + 1
                shard = lax.div(column, SLAB_DEV)
                at = plan.length(place, shard)
                length = plan_ref[at]
                plan_ref[plan.entry(place, shard, length)] = k * SLAB_DEV + column - shard * SLAB_DEV
                plan_ref[at] = length + 1

            return carry

        lax.fori_loop(0, rows, one, 0)
    for copy in copies:
        copy.wait()
    total[...] = jnp.zeros_like(total)

    @pl.when(jnp.logical_not(is_inner()))
    def _():
        for place, held in enumerate((own_near, twin)):
            add_terms(plan, which(lax.axis_index("col")), place, held, total, operand_near)


def add_terms(plan, shard, place, held, total, operand):
    length = plan.ref[plan.length(place, shard)]

    def term(j):
        entry = jnp.where(j < length, plan.ref[plan.entry(place, shard, jnp.minimum(j, plan.rows - 1))], 0)
        k, column = lax.div(entry, SLAB_DEV), lax.rem(entry, SLAB_DEV)
        block = held[k, 0]
        block = jnp.where(j < length, block, jnp.zeros_like(block))
        left = operand[:, pl.ds(pl.multiple_of(k * SIDE, SIDE), SIDE)]
        lanes = pl.ds(pl.multiple_of(column * SIDE, SIDE), SIDE)
        return lanes, jnp.dot(left, block, preferred_element_type=jnp.float32)

    def step(some, carry):
        for lanes, value in [term(ABREAST * some + j) for j in range(ABREAST)]:
            total[:, lanes] = total[:, lanes] + value
        return carry

    lax.fori_loop(0, lax.div(length + ABREAST - 1, ABREAST), step, 0)


def go_on(which, place, plan_ref, operand, held, _, total):
    @pl.when(jnp.logical_not(is_inner()))
    def _():
        add_terms(plan_of(plan_ref, operand), which(lax.axis_index("col")), place, held, total, operand)


def code_sum(which, place, plan_ref, operand, held, total, out):
    plan = plan_of(plan_ref, operand)
    shard = which(lax.axis_index("col"))

    @pl.when(is_inner())
    def _():
        out[...] = jnp.zeros_like(out)

    @pl.when(jnp.logical_not(is_inner()))
    def _():
        add_terms(plan, shard, place, held, total, operand)
        values = [(b, lambda b=b: total[:, lanes_of(b)]) for b in range(SLAB_DEV)]
        put_coded([(out, ALL)], values, counts_of(plan, shard))


def fill(slab, plan, shard, blocks):
    slab[...] = jnp.zeros_like(slab)
    for place, held in enumerate(blocks):

        def one(j, carry, place=place, held=held):
            entry = plan.ref[plan.entry(place, shard, j)]
            k, column = lax.div(entry, SLAB_DEV), lax.rem(entry, SLAB_DEV)
            where = (pl.ds(pl.multiple_of(k * SIDE, SIDE), SIDE), pl.ds(pl.multiple_of(column * SIDE, SIDE), SIDE))
            slab[where] = held[k, 0]
            return carry

        lax.fori_loop(0, plan.ref[plan.length(place, shard)], one, 0)


def counts_of(plan, shard):
    row = lax.broadcasted_iota(jnp.int32, (HEAD, SIDE), 0)
    head = jnp.zeros((HEAD, SIDE), jnp.int32)
    for b in range(SLAB_DEV):
        head = jnp.where(row == SLAB_DEV + b, plan.ref[plan.load(shard * SLAB_DEV + b)], head)
    return head


def tiles(width, body):
    def step(tile, carry):
        body(tile, pl.ds(pl.multiple_of(tile * TILE, TILE), TILE))
        return carry

    lax.fori_loop(0, width // TILE, step, 0)


def coded_product(which, helds, nblocks, plan_ref, operand, *refs):
    blocks, (*outs, slab) = refs[:nblocks], refs[nblocks:]
    plan = plan_of(plan_ref, operand)
    shard = which(lax.axis_index("col"))
    fill(slab, plan, shard, blocks)
    done = {}

    def values(block):
        tile, at = block * SIDE // TILE, block * SIDE % TILE
        if tile not in done:
            lanes = pl.ds(tile * TILE, TILE)
            done[tile] = jnp.dot(operand[...], slab[:, lanes], preferred_element_type=jnp.float32)
        return done[tile][:, at : at + SIDE]

    put_coded(list(zip(outs, helds)), [(b, functools.partial(values, b)) for b in ALL], counts_of(plan, shard))


def plain_products(plain, nblocks, plan_ref, operand, *refs):
    blocks, (*outs, slab) = refs[:nblocks], refs[nblocks:]
    outs, loads = outs[: len(plain)], outs[len(plain) :]
    plan = plan_of(plan_ref, operand)
    for which, out, row in zip(plain, outs, loads):
        shard = which(lax.axis_index("col"))
        fill(slab, plan, shard, blocks)

        def body(tile, lanes, out=out):
            out[:, lanes] = jnp.dot(operand[...], slab[:, lanes], preferred_element_type=jnp.float32)

        tiles(slab.shape[1], body)
        row[...] = counts_of(plan, shard)


def relay(part, own, own_load, came, out):
    inner = is_inner()
    held, rows = blocks_of(part), own.shape[0]

    @pl.when(inner)
    def _():
        head = head_of(came)
        values = [
            (b, lambda at=at, b=b: own[:, lanes_of(b)] + decode(came, head, at, rows)) for at, b in enumerate(held)
        ]
        put_coded([(out, held)], values, own_load[...] + head)

    @pl.when(jnp.logical_not(inner))
    def _():
        put_coded([(out, held)], [(b, lambda b=b: own[:, lanes_of(b)]) for b in held], own_load[...])


def settle(own, own_load, *refs):
    *came_a, came_b, came_f, out, out_load = refs
    rows = own.shape[0]

    @pl.when(is_inner())
    def _():
        head_b, head_f = head_of(came_b), head_of(came_f)
        out_load[...] = own_load[...] + head_b + head_f
        for b in ALL:
            came = decode(came_b, head_b, b, rows) + decode(came_f, head_f, b, rows)
            out[:, lanes_of(b)] = own[:, lanes_of(b)] + came

    @pl.when(jnp.logical_not(is_inner()))
    def _():
        out_load[...] = own_load[...] + head_of(came_a[0])
        for part, came in enumerate(came_a):
            head = head_of(came)
            for at, b in enumerate(blocks_of(part)):
                out[:, lanes_of(b)] = own[:, lanes_of(b)] + decode(came, head, at, rows)


def inflate(part, own, came, out, totals):
    rows, head = own.shape[0], head_of(came)
    for at, b in enumerate(blocks_of(part)):
        expanded = own[:, lanes_of(b)] + decode(came, head, at, rows)
        inflated = expanded * expanded
        out[:, lanes_of(at)] = inflated
        totals[:, lanes_of(at)] = jnp.sum(inflated.reshape(-1, 8, SIDE), axis=0)


def count(own_load, came, load):
    head = own_load[...] + head_of(came)
    for j in range(SLAB_DEV):
        load[j] = jnp.max(head[SLAB_DEV + j : SLAB_DEV + j + 1])


def scale(all_rows, part, inflated, *refs):
    *totals, out, scaled, sems = refs[:-4] + refs[-3:] if part else refs
    rows, width = inflated.shape
    total = totals[0][...]
    for other in totals[1:]:
        total = total + other[...]
    total = jnp.sum(total, axis=0, keepdims=True)
    factor = 1.0 / (total / all_rows + 1e-06)
    few = rows // sems.shape[0]
    copies = []
    for j in range(sems.shape[0]):
        these = pl.ds(j * few, few)
        scaled[these, :] = inflated[these, :] * factor
        copy = pltpu.make_async_copy(scaled.at[these, :], out.at[these, pl.ds(part * width, width)], sems.at[j])
        copy.start()
        copies.append(copy)
    for copy in copies:
        copy.wait()


def call(kernel, ins, out_shape, out_specs, scratch=(), flops=0, few=0, far=0, onto=None, last=False):
    moved = sum(x.size * x.dtype.itemsize for x in list(ins) + list(out_shape))
    return pl.pallas_call(
        kernel,
        in_specs=[SMEM] * few + [pl.BlockSpec(memory_space=pltpu.HBM)] * far + [VMEM] * (len(ins) - few - far - last) + [pl.BlockSpec(memory_space=pl.ANY)] * last,
        out_shape=out_shape,
        out_specs=out_specs,
        scratch_shapes=list(scratch),
        input_output_aliases=onto or {},
        compiler_params=pltpu.CompilerParams(vmem_limit_bytes=24 << 20),
        cost_estimate=pl.CostEstimate(flops=flops // COST, bytes_accessed=moved // COST, transcendentals=0),
    )(*ins)


def body_line(operand_panel, slot_blocks, slot_columns, live_counts):
    ny = lax.axis_size("row") // 2
    rows, depth = operand_panel.shape
    here, slots = slot_columns.shape
    width = SLAB_DEV * SIDE
    shards = lax.axis_size("col")
    f32 = functools.partial(jax.ShapeDtypeStruct, dtype=jnp.float32)
    i32 = functools.partial(jax.ShapeDtypeStruct, dtype=jnp.int32)
    coded = jax.ShapeDtypeStruct((SLAB_DEV * rows + HEAD, SIDE), jnp.int16)

    swap = [(a, a ^ 1) for a in range(2 * ny)]

    def turn(by):
        return [(a, ((a // 2 + by) % ny) * 2 + a % 2) for a in range(2 * ny)]

    def first(z):
        return jnp.where(z == 0, 2, 1)

    def second(z):
        return jnp.where(lax.rem(z, 2) == 0, 3, 0)

    def inner(z):
        return jnp.where(z < 2, 2, 1)

    def third(z):
        return jnp.where(z == 0, 1, jnp.where(z == 1, 3, jnp.where(z == 2, 0, 2)))

    flops = 2 * rows * depth * width
    turned = [lax.ppermute(slot_blocks, "row", turn(by)) for by in range(1, ny)]
    twin = lax.ppermute(slot_blocks, "row", swap)
    plan, operand_near, own_near, total = call(
        functools.partial(begin, ny, first),
        [slot_columns.T, live_counts, operand_panel, slot_blocks, twin],
        [
            i32((Plan(None, here, slots, shards).size,)),
            jax.ShapeDtypeStruct(operand_panel.shape, operand_panel.dtype),
            jax.ShapeDtypeStruct(slot_blocks.shape, slot_blocks.dtype),
            f32((rows, width)),
        ],
        [SMEM] + [VMEM] * 3,
        [pltpu.SemaphoreType.DMA((2,))],
        flops // 4,
        few=2,
        far=2,
    )
    turned, plan = lax.optimization_barrier((turned, plan))
    blocks = [own_near, twin]
    blocks += [x for came in turned for x in (came, lax.ppermute(came, "row", swap))]
    for place in range(2, slots - 1):
        [total] = call(
            functools.partial(go_on, first, place),
            [plan, operand_near, blocks[place], total],
            [f32((rows, width))],
            [VMEM],
            (),
            flops // 8,
            1,
            onto={3: 0},
        )
    [send_f] = call(
        functools.partial(code_sum, first, slots - 1),
        [plan, operand_near, blocks[-1], total],
        [coded],
        [VMEM],
        (),
        flops // 8,
        1,
    )
    came_f = lax.ppermute(send_f, "col", [(0, 2), (1, 0), (2, 3), (3, 1)])
    ins = [plan, operand_near, *blocks]
    slab = [pltpu.VMEM((depth, width), jnp.bfloat16)]
    part_coded = jax.ShapeDtypeStruct((SLAB_DEV // PARTS * rows + HEAD, SIDE), jnp.int16)
    send_a = call(
        functools.partial(coded_product, second, [blocks_of(j) for j in range(PARTS)], len(blocks)),
        ins,
        [part_coded] * PARTS,
        [VMEM] * PARTS,
        slab,
        flops,
        1,
    )
    came_a = [lax.ppermute(one, "col", [(0, 1), (1, 0), (2, 3), (3, 2)]) for one in send_a]
    [send_b] = call(
        functools.partial(coded_product, inner, [ALL], len(blocks)), ins, [coded], [VMEM], slab, flops, 1
    )
    came_b = lax.ppermute(
        send_b,
        ("row", "col"),
        [(4 * r + c, 4 * r + 3 - c if c in (1, 2) else 4 * (r ^ 1) + c) for r in range(2 * ny) for c in range(4)],
    )
    ins[0], came_f = lax.optimization_barrier((ins[0], came_f))
    passed, own, passed_load, own_load = call(
        functools.partial(plain_products, (third, lambda z: z), len(blocks)),
        ins,
        [f32((rows, width)), f32((rows, width)), i32((HEAD, SIDE)), i32((HEAD, SIDE))],
        [VMEM] * 4,
        slab,
        2 * flops,
        1,
    )
    came_a[-1], came_b = lax.optimization_barrier((came_a[-1], came_b))
    came_t = []
    for part in range(PARTS):
        [send_t] = call(
            functools.partial(relay, part), [passed, passed_load, came_a[part]], [part_coded], [VMEM]
        )
        came_t.append(lax.ppermute(send_t, "col", [(0, 1), (1, 3), (3, 2), (2, 0)]))
    own, own_load = call(
        settle, [own, own_load, *came_a, came_b, came_f], [f32((rows, width)), i32((HEAD, SIDE))], [VMEM] * 2
    )
    all_rows = rows * lax.axis_size("row")
    hbm = pl.BlockSpec(memory_space=pl.ANY)
    result = []
    [load] = call(count, [own_load, came_t[0]], [i32((SLAB_DEV,))], [SMEM])
    for part in range(PARTS):
        inflated, totals = call(
            functools.partial(inflate, part),
            [own, came_t[part]],
            [f32((rows, width // PARTS)), f32((8, width // PARTS))],
            [VMEM] * 2,
        )
        others = [totals]
        for by in range(ny):
            for flip in (0, 1):
                if by or flip:
                    pairs = [(a, ((a // 2 + by) % ny) * 2 + (a % 2 ^ flip)) for a in range(2 * ny)]
                    others.append(lax.ppermute(totals, "row", pairs))
        result = call(
            functools.partial(scale, all_rows, part),
            [inflated, *others, *result],
            [f32((rows, width))],
            [hbm],
            [pltpu.VMEM((rows, width // PARTS), jnp.float32), pltpu.SemaphoreType.DMA((4,))],
            onto={1 + len(others): 0} if part else None,
            last=bool(part),
        )
    return result[0], load


def densify(blocks, columns, counts, first_row, slab_width):
    rows_here, slots = columns.shape
    side = blocks.shape[2]
    places = jnp.arange(slots, dtype=jnp.int32)
    rows_index = first_row + jnp.arange(rows_here, dtype=jnp.int32)
    live = jnp.mod(places[None, :] - rows_index[:, None], slots) < counts[:, None]
    onehot = (columns[:, :, None] == jnp.arange(slab_width, dtype=jnp.int32)[None, None, :]) & live[:, :, None]
    dense = jnp.einsum(
        "kej,kebc->kbjc", onehot.astype(jnp.bfloat16), blocks, preferred_element_type=jnp.float32
    )
    dense = dense.astype(jnp.bfloat16).reshape(rows_here * side, slab_width * side)
    return (dense, jnp.sum(onehot.astype(jnp.float32), axis=(0, 1)))


def body_any(operand_panel, slot_blocks, slot_columns, live_counts):
    gathered = lax.all_gather(slot_blocks, "row", axis=1, tiled=True)
    slab_width = SLAB_DEV * lax.axis_size("col")
    first_row = lax.axis_index("col") * slot_columns.shape[0]
    dense, load = densify(gathered, slot_columns, live_counts, first_row, slab_width)
    partial_terms = jnp.dot(operand_panel, dense, preferred_element_type=jnp.float32)
    expanded, load_mine = (
        lax.psum_scatter(partial_terms, "col", scatter_dimension=1, tiled=True),
        lax.psum_scatter(load, "col", scatter_dimension=0, tiled=True),
    )
    inflated = expanded * expanded
    totals = lax.psum(jnp.sum(inflated, axis=0), "row")
    all_rows = expanded.shape[0] * lax.axis_size("row")
    mcl_columns = inflated / (totals / all_rows + 1e-06)
    return (mcl_columns, load_mine.astype(jnp.int32))


def solution(mesh):
    placed = (
        P(("groups", "row"), "col"),
        P(("groups", "col"), "row", None, None),
        P(("groups", "col"), None),
        P(("groups", "col")),
    )
    return jax.shard_map(
        body_line if mesh.shape["col"] == 4 else body_any,
        mesh=mesh,
        in_specs=placed,
        out_specs=(P(("groups", "row"), "col"), P(("groups", "col"))),
        check_vma=False,
    )
```

```python
import functools

import jax
import jax.numpy as jnp
from jax import lax
from jax.experimental import pallas as pl
from jax.experimental.pallas import tpu as pltpu
from jax.sharding import PartitionSpec as P

SLAB_DEV = 4
SIDE = 128
HEAD = 16
TILE = 256
ABREAST = 4
PARTS = 2
COST = 1
STEPS = 32700.0
NEAREST = 12582912.0
OCTAVE = 128.0

ALL = list(range(SLAB_DEV))

VMEM = pl.BlockSpec(memory_space=pltpu.VMEM)
SMEM = pl.BlockSpec(memory_space=pltpu.SMEM)


def blocks_of(part):
    return ALL[part * SLAB_DEV // PARTS : (part + 1) * SLAB_DEV // PARTS]


def code_scale(values):
    most = jnp.max(jnp.abs(values), axis=0, keepdims=True)
    octaves = jnp.log2(jnp.maximum(most, 1e-30))
    return jnp.ceil(octaves * OCTAVE)


def encode(values, code):
    scaled = values * (STEPS * jnp.exp2(code * (-1.0 / OCTAVE)))
    return ((scaled + NEAREST) - NEAREST).astype(jnp.int32).astype(jnp.int16)


def put_coded(outs, values, counts):
    row = lax.broadcasted_iota(jnp.int32, counts.shape, 0)
    heads = [jnp.where(row < SLAB_DEV, 0, counts) for _ in outs]
    for block, get in values:
        value = get()
        rows = value.shape[0]
        code = code_scale(value)
        coded = encode(value, code)
        for j, (out, held) in enumerate(outs):
            if block in held:
                at = held.index(block)
                out[pl.ds(at * rows, rows), :] = coded
                heads[j] = jnp.where(row == at, jnp.broadcast_to(code.astype(jnp.int32), counts.shape), heads[j])
    for (out, _), head in zip(outs, heads):
        out[pl.ds(out.shape[0] - HEAD, HEAD), :] = head.astype(jnp.int16)


def head_of(ref):
    return ref[pl.ds(ref.shape[0] - HEAD, HEAD), :].astype(jnp.int32)


def decode(ref, head, at, rows):
    scale = jnp.exp2(head[at : at + 1].astype(jnp.float32) * (1.0 / OCTAVE)) * (1.0 / STEPS)
    return ref[pl.ds(at * rows, rows), :].astype(jnp.int32).astype(jnp.float32) * scale


def lanes_of(block):
    return pl.ds(block * SIDE, SIDE)


def slot_of(place, ny):
    me = lax.axis_index("row")
    y, core = lax.div(me, 2), lax.rem(me, 2)
    return lax.rem(y + ny - place // 2, ny) * 2 + (core if place % 2 == 0 else 1 - core)


def is_live(columns, counts, k, e):
    slots, rows = columns.shape
    row_index = lax.axis_index("col") * rows + k
    all_rows = rows * lax.axis_size("col")
    return lax.rem(e - row_index + all_rows * slots, slots) < counts[k]


class Plan:
    def __init__(self, ref, rows, slots, shards):
        self.ref, self.rows, self.slots, self.shards = ref, rows, slots, shards
        self.lens = rows * slots * shards
        self.loads = self.lens + slots * shards
        self.size = self.loads + SLAB_DEV * shards

    def entry(self, place, shard, j):
        return (place * self.shards + shard) * self.rows + j

    def length(self, place, shard):
        return self.lens + place * self.shards + shard

    def load(self, column):
        return self.loads + column


def plan_of(ref, operand):
    rows = operand.shape[1] // SIDE
    return Plan(ref, rows, lax.axis_size("row"), lax.axis_size("col"))


def begin(ny, which, columns, counts, operand, own, twin, plan_ref, operand_near, own_near, total, sems):
    copies = [
        pltpu.make_async_copy(far, near, sems.at[j])
        for j, (far, near) in enumerate(((operand, operand_near), (own, own_near)))
    ]
    for copy in copies:
        copy.start()
    slots, rows = columns.shape
    plan = plan_of(plan_ref, operand)

    def clear(j, carry):
        plan_ref[plan.lens + j] = 0
        return carry

    lax.fori_loop(0, plan.size - plan.lens, clear, 0)
    for place in range(slots):
        e = slot_of(place, ny)

        def one(k, carry, place=place, e=e):
            @pl.when(is_live(columns, counts, k, e))
            def _():
                column = columns[e, k]
                plan_ref[plan.load(column)] = plan_ref[plan.load(column)] + 1
                shard = lax.div(column, SLAB_DEV)
                at = plan.length(place, shard)
                length = plan_ref[at]
                plan_ref[plan.entry(place, shard, length)] = k * SLAB_DEV + column - shard * SLAB_DEV
                plan_ref[at] = length + 1

            return carry

        lax.fori_loop(0, rows, one, 0)
    for copy in copies:
        copy.wait()
    total[...] = jnp.zeros_like(total)
    for place, held in enumerate((own_near, twin)):
        add_terms(plan, which(lax.axis_index("col")), place, held, total, operand_near)


def add_terms(plan, shard, place, held, total, operand):
    length = plan.ref[plan.length(place, shard)]

    def term(j):
        entry = jnp.where(j < length, plan.ref[plan.entry(place, shard, jnp.minimum(j, plan.rows - 1))], 0)
        k, column = lax.div(entry, SLAB_DEV), lax.rem(entry, SLAB_DEV)
        block = held[k, 0]
        block = jnp.where(j < length, block, jnp.zeros_like(block))
        left = operand[:, pl.ds(pl.multiple_of(k * SIDE, SIDE), SIDE)]
        lanes = pl.ds(pl.multiple_of(column * SIDE, SIDE), SIDE)
        return lanes, jnp.dot(left, block, preferred_element_type=jnp.float32)

    def step(some, carry):
        for lanes, value in [term(ABREAST * some + j) for j in range(ABREAST)]:
            total[:, lanes] = total[:, lanes] + value
        return carry

    lax.fori_loop(0, lax.div(length + ABREAST - 1, ABREAST), step, 0)


def go_on(which, place, plan_ref, operand, held, _, total):
    add_terms(plan_of(plan_ref, operand), which(lax.axis_index("col")), place, held, total, operand)


def code_sum(which, place, plan_ref, operand, held, total, out):
    plan = plan_of(plan_ref, operand)
    shard = which(lax.axis_index("col"))
    add_terms(plan, shard, place, held, total, operand)
    values = [(b, lambda b=b: total[:, lanes_of(b)]) for b in range(SLAB_DEV)]
    put_coded([(out, ALL)], values, counts_of(plan, shard))


def fill(slab, plan, shard, blocks):
    slab[...] = jnp.zeros_like(slab)
    for place, held in enumerate(blocks):

        def one(j, carry, place=place, held=held):
            entry = plan.ref[plan.entry(place, shard, j)]
            k, column = lax.div(entry, SLAB_DEV), lax.rem(entry, SLAB_DEV)
            where = (pl.ds(pl.multiple_of(k * SIDE, SIDE), SIDE), pl.ds(pl.multiple_of(column * SIDE, SIDE), SIDE))
            slab[where] = held[k, 0]
            return carry

        lax.fori_loop(0, plan.ref[plan.length(place, shard)], one, 0)


def counts_of(plan, shard):
    row = lax.broadcasted_iota(jnp.int32, (HEAD, SIDE), 0)
    head = jnp.zeros((HEAD, SIDE), jnp.int32)
    for b in range(SLAB_DEV):
        head = jnp.where(row == SLAB_DEV + b, plan.ref[plan.load(shard * SLAB_DEV + b)], head)
    return head


def tiles(width, body):
    def step(tile, carry):
        body(tile, pl.ds(pl.multiple_of(tile * TILE, TILE), TILE))
        return carry

    lax.fori_loop(0, width // TILE, step, 0)


def coded_product(which, nblocks, plan_ref, operand, *refs):
    blocks, (whole, *parts, slab) = refs[:nblocks], refs[nblocks:]
    plan = plan_of(plan_ref, operand)
    shard = which(lax.axis_index("col"))
    fill(slab, plan, shard, blocks)
    done = {}

    def values(block):
        tile, at = block * SIDE // TILE, block * SIDE % TILE
        if tile not in done:
            lanes = pl.ds(tile * TILE, TILE)
            done[tile] = jnp.dot(operand[...], slab[:, lanes], preferred_element_type=jnp.float32)
        return done[tile][:, at : at + SIDE]

    outs = [(whole, ALL)] + [(part, blocks_of(j)) for j, part in enumerate(parts)]
    put_coded(outs, [(b, functools.partial(values, b)) for b in ALL], counts_of(plan, shard))


def plain_products(plain, nblocks, plan_ref, operand, *refs):
    blocks, (*outs, slab) = refs[:nblocks], refs[nblocks:]
    outs, loads = outs[: len(plain)], outs[len(plain) :]
    plan = plan_of(plan_ref, operand)
    for which, out, row in zip(plain, outs, loads):
        shard = which(lax.axis_index("col"))
        fill(slab, plan, shard, blocks)

        def body(tile, lanes, out=out):
            out[:, lanes] = jnp.dot(operand[...], slab[:, lanes], preferred_element_type=jnp.float32)

        tiles(slab.shape[1], body)
        row[...] = counts_of(plan, shard)


def relay(part, own, own_load, came, out):
    place = lax.axis_index("col")
    inner = (place == 1) | (place == 2)
    held, rows = blocks_of(part), own.shape[0]

    @pl.when(inner)
    def _():
        head = head_of(came)
        values = [
            (b, lambda at=at, b=b: own[:, lanes_of(b)] + decode(came, head, at, rows)) for at, b in enumerate(held)
        ]
        put_coded([(out, held)], values, own_load[...] + head)

    @pl.when(jnp.logical_not(inner))
    def _():
        put_coded([(out, held)], [(b, lambda b=b: own[:, lanes_of(b)]) for b in held], own_load[...])


def settle(own, own_load, came_b, came_f, out, out_load):
    place = lax.axis_index("col")
    inner = (place == 1) | (place == 2)
    rows, head = own.shape[0], head_of(came_f)
    out_load[...] = own_load[...] + head
    for b in ALL:
        out[:, lanes_of(b)] = own[:, lanes_of(b)] + decode(came_f, head, b, rows)

    @pl.when(inner)
    def _():
        head = head_of(came_b)
        out_load[...] = out_load[...] + head
        for b in ALL:
            out[:, lanes_of(b)] = out[:, lanes_of(b)] + decode(came_b, head, b, rows)


def inflate(part, own, came, out, totals):
    rows, head = own.shape[0], head_of(came)
    for at, b in enumerate(blocks_of(part)):
        expanded = own[:, lanes_of(b)] + decode(came, head, at, rows)
        inflated = expanded * expanded
        out[:, lanes_of(at)] = inflated
        totals[:, lanes_of(at)] = jnp.sum(inflated.reshape(-1, 8, SIDE), axis=0)


def count(own_load, came, load):
    head = own_load[...] + head_of(came)
    for j in range(SLAB_DEV):
        load[j] = jnp.max(head[SLAB_DEV + j : SLAB_DEV + j + 1])


def scale(all_rows, part, inflated, *refs):
    *totals, out, scaled, sems = refs[:-4] + refs[-3:] if part else refs
    rows, width = inflated.shape
    total = totals[0][...]
    for other in totals[1:]:
        total = total + other[...]
    total = jnp.sum(total, axis=0, keepdims=True)
    factor = 1.0 / (total / all_rows + 1e-06)
    few = rows // sems.shape[0]
    copies = []
    for j in range(sems.shape[0]):
        these = pl.ds(j * few, few)
        scaled[these, :] = inflated[these, :] * factor
        copy = pltpu.make_async_copy(scaled.at[these, :], out.at[these, pl.ds(part * width, width)], sems.at[j])
        copy.start()
        copies.append(copy)
    for copy in copies:
        copy.wait()


def call(kernel, ins, out_shape, out_specs, scratch=(), flops=0, few=0, far=0, onto=None, last=False):
    moved = sum(x.size * x.dtype.itemsize for x in list(ins) + list(out_shape))
    return pl.pallas_call(
        kernel,
        in_specs=[SMEM] * few + [pl.BlockSpec(memory_space=pltpu.HBM)] * far + [VMEM] * (len(ins) - few - far - last) + [pl.BlockSpec(memory_space=pl.ANY)] * last,
        out_shape=out_shape,
        out_specs=out_specs,
        scratch_shapes=list(scratch),
        input_output_aliases=onto or {},
        compiler_params=pltpu.CompilerParams(vmem_limit_bytes=24 << 20),
        cost_estimate=pl.CostEstimate(flops=flops // COST, bytes_accessed=moved // COST, transcendentals=0),
    )(*ins)


def body_line(operand_panel, slot_blocks, slot_columns, live_counts):
    ny = lax.axis_size("row") // 2
    rows, depth = operand_panel.shape
    here, slots = slot_columns.shape
    width = SLAB_DEV * SIDE
    shards = lax.axis_size("col")
    f32 = functools.partial(jax.ShapeDtypeStruct, dtype=jnp.float32)
    i32 = functools.partial(jax.ShapeDtypeStruct, dtype=jnp.int32)
    coded = jax.ShapeDtypeStruct((SLAB_DEV * rows + HEAD, SIDE), jnp.int16)

    swap = [(a, a ^ 1) for a in range(2 * ny)]

    def turn(by):
        return [(a, ((a // 2 + by) % ny) * 2 + a % 2) for a in range(2 * ny)]

    def first(z):
        return 3 - z

    def second(z):
        return jnp.where(z == 0, 2, jnp.where(z == 1, 0, jnp.where(z == 2, 3, 1)))

    def third(z):
        return 3 - second(z)

    flops = 2 * rows * depth * width
    turned = [lax.ppermute(slot_blocks, "row", turn(by)) for by in range(1, ny)]
    twin = lax.ppermute(slot_blocks, "row", swap)
    plan, operand_near, own_near, total = call(
        functools.partial(begin, ny, second),
        [slot_columns.T, live_counts, operand_panel, slot_blocks, twin],
        [
            i32((Plan(None, here, slots, shards).size,)),
            jax.ShapeDtypeStruct(operand_panel.shape, operand_panel.dtype),
            jax.ShapeDtypeStruct(slot_blocks.shape, slot_blocks.dtype),
            f32((rows, width)),
        ],
        [SMEM] + [VMEM] * 3,
        [pltpu.SemaphoreType.DMA((2,))],
        flops // 4,
        few=2,
        far=2,
    )
    turned, plan = lax.optimization_barrier((turned, plan))
    blocks = [own_near, twin]
    blocks += [x for came in turned for x in (came, lax.ppermute(came, "row", swap))]
    for place in range(2, slots - 1):
        [total] = call(
            functools.partial(go_on, second, place),
            [plan, operand_near, blocks[place], total],
            [f32((rows, width))],
            [VMEM],
            (),
            flops // 8,
            1,
            onto={3: 0},
        )
    [send_f] = call(
        functools.partial(code_sum, second, slots - 1),
        [plan, operand_near, blocks[-1], total],
        [coded],
        [VMEM],
        (),
        flops // 8,
        1,
    )
    came_f = lax.ppermute(send_f, "col", [(0, 2), (1, 0), (2, 3), (3, 1)])
    ins = [plan, operand_near, *blocks]
    slab = [pltpu.VMEM((depth, width), jnp.bfloat16)]
    part_coded = jax.ShapeDtypeStruct((SLAB_DEV // PARTS * rows + HEAD, SIDE), jnp.int16)
    send_b, *send_a = call(
        functools.partial(coded_product, first, len(blocks)),
        ins,
        [coded] + [part_coded] * PARTS,
        [VMEM] * (1 + PARTS),
        slab,
        flops,
        1,
    )
    came_a = [lax.ppermute(one, "col", [(0, 1), (1, 0), (2, 3), (3, 2)]) for one in send_a]
    came_b = lax.ppermute(
        send_b,
        ("row", "col"),
        [(4 * r + c, 4 * r + 3 - c if c in (1, 2) else 4 * (r ^ 1) + c) for r in range(2 * ny) for c in range(4)],
    )
    ins[0], came_f = lax.optimization_barrier((ins[0], came_f))
    passed, own, passed_load, own_load = call(
        functools.partial(plain_products, (third, lambda z: z), len(blocks)),
        ins,
        [f32((rows, width)), f32((rows, width)), i32((HEAD, SIDE)), i32((HEAD, SIDE))],
        [VMEM] * 4,
        slab,
        2 * flops,
        1,
    )
    came_a[-1], came_b = lax.optimization_barrier((came_a[-1], came_b))
    came_t = []
    for part in range(PARTS):
        [send_t] = call(
            functools.partial(relay, part), [passed, passed_load, came_a[part]], [part_coded], [VMEM]
        )
        came_t.append(lax.ppermute(send_t, "col", [(0, 1), (1, 3), (3, 2), (2, 0)]))
    own, own_load = call(
        settle, [own, own_load, came_b, came_f], [f32((rows, width)), i32((HEAD, SIDE))], [VMEM] * 2
    )
    all_rows = rows * lax.axis_size("row")
    hbm = pl.BlockSpec(memory_space=pl.ANY)
    result = []
    [load] = call(count, [own_load, came_t[0]], [i32((SLAB_DEV,))], [SMEM])
    for part in range(PARTS):
        inflated, totals = call(
            functools.partial(inflate, part),
            [own, came_t[part]],
            [f32((rows, width // PARTS)), f32((8, width // PARTS))],
            [VMEM] * 2,
        )
        others = [totals]
        steps = [(by, 1) for by in range(1, ny)] + [(by, 0) for by in range(1, ny)] + [(0, 1)]
        for by, flip in steps:
            pairs = [(a, ((a // 2 + by) % ny) * 2 + (a % 2 ^ flip)) for a in range(2 * ny)]
            others.append(lax.ppermute(totals, "row", pairs))
        result = call(
            functools.partial(scale, all_rows, part),
            [inflated, *others, *result],
            [f32((rows, width))],
            [hbm],
            [pltpu.VMEM((rows, width // PARTS), jnp.float32), pltpu.SemaphoreType.DMA((4,))],
            onto={1 + len(others): 0} if part else None,
            last=bool(part),
        )
    return result[0], load


def densify(blocks, columns, counts, first_row, slab_width):
    rows_here, slots = columns.shape
    side = blocks.shape[2]
    places = jnp.arange(slots, dtype=jnp.int32)
    rows_index = first_row + jnp.arange(rows_here, dtype=jnp.int32)
    live = jnp.mod(places[None, :] - rows_index[:, None], slots) < counts[:, None]
    onehot = (columns[:, :, None] == jnp.arange(slab_width, dtype=jnp.int32)[None, None, :]) & live[:, :, None]
    dense = jnp.einsum(
        "kej,kebc->kbjc", onehot.astype(jnp.bfloat16), blocks, preferred_element_type=jnp.float32
    )
    dense = dense.astype(jnp.bfloat16).reshape(rows_here * side, slab_width * side)
    return (dense, jnp.sum(onehot.astype(jnp.float32), axis=(0, 1)))


def body_any(operand_panel, slot_blocks, slot_columns, live_counts):
    gathered = lax.all_gather(slot_blocks, "row", axis=1, tiled=True)
    slab_width = SLAB_DEV * lax.axis_size("col")
    first_row = lax.axis_index("col") * slot_columns.shape[0]
    dense, load = densify(gathered, slot_columns, live_counts, first_row, slab_width)
    partial_terms = jnp.dot(operand_panel, dense, preferred_element_type=jnp.float32)
    expanded, load_mine = (
        lax.psum_scatter(partial_terms, "col", scatter_dimension=1, tiled=True),
        lax.psum_scatter(load, "col", scatter_dimension=0, tiled=True),
    )
    inflated = expanded * expanded
    totals = lax.psum(jnp.sum(inflated, axis=0), "row")
    all_rows = expanded.shape[0] * lax.axis_size("row")
    mcl_columns = inflated / (totals / all_rows + 1e-06)
    return (mcl_columns, load_mine.astype(jnp.int32))


def solution(mesh):
    placed = (
        P(("groups", "row"), "col"),
        P(("groups", "col"), "row", None, None),
        P(("groups", "col"), None),
        P(("groups", "col")),
    )
    return jax.shard_map(
        body_line if mesh.shape["col"] == 4 else body_any,
        mesh=mesh,
        in_specs=placed,
        out_specs=(P(("groups", "row"), "col"), P(("groups", "col"))),
        check_vma=False,
    )
```

```python
import functools

import jax
import jax.numpy as jnp
from jax import lax
from jax.experimental import pallas as pl
from jax.experimental.pallas import tpu as pltpu
from jax.sharding import PartitionSpec as P

SLAB_DEV = 4
SIDE = 128
HEAD = 16
TILE = 256
ABREAST = 4
PARTS = 2
COST = 1
STEPS = 32700.0
NEAREST = 12582912.0
OCTAVE = 128.0

ALL = list(range(SLAB_DEV))

VMEM = pl.BlockSpec(memory_space=pltpu.VMEM)
SMEM = pl.BlockSpec(memory_space=pltpu.SMEM)


def blocks_of(part):
    return ALL[part * SLAB_DEV // PARTS : (part + 1) * SLAB_DEV // PARTS]


def is_inner():
    place = lax.axis_index("col")
    return (place == 1) | (place == 2)


def code_scale(values):
    most = jnp.max(jnp.abs(values), axis=0, keepdims=True)
    octaves = jnp.log2(jnp.maximum(most, 1e-30))
    return jnp.ceil(octaves * OCTAVE)


def encode(values, code):
    scaled = values * (STEPS * jnp.exp2(code * (-1.0 / OCTAVE)))
    return ((scaled + NEAREST) - NEAREST).astype(jnp.int32).astype(jnp.int16)


def put_coded(outs, values, counts):
    row = lax.broadcasted_iota(jnp.int32, counts.shape, 0)
    heads = [jnp.where(row < SLAB_DEV, 0, counts) for _ in outs]
    for block, get in values:
        value = get()
        rows = value.shape[0]
        code = code_scale(value)
        coded = encode(value, code)
        for j, (out, held) in enumerate(outs):
            if block in held:
                at = held.index(block)
                out[pl.ds(at * rows, rows), :] = coded
                heads[j] = jnp.where(row == at, jnp.broadcast_to(code.astype(jnp.int32), counts.shape), heads[j])
    for (out, _), head in zip(outs, heads):
        out[pl.ds(out.shape[0] - HEAD, HEAD), :] = head.astype(jnp.int16)


def head_of(ref):
    return ref[pl.ds(ref.shape[0] - HEAD, HEAD), :].astype(jnp.int32)


def decode(ref, head, at, rows):
    scale = jnp.exp2(head[at : at + 1].astype(jnp.float32) * (1.0 / OCTAVE)) * (1.0 / STEPS)
    return ref[pl.ds(at * rows, rows), :].astype(jnp.int32).astype(jnp.float32) * scale


def lanes_of(block):
    return pl.ds(block * SIDE, SIDE)


def slot_of(place, ny):
    me = lax.axis_index("row")
    y, core = lax.div(me, 2), lax.rem(me, 2)
    return lax.rem(y + ny - place // 2, ny) * 2 + (core if place % 2 == 0 else 1 - core)


def is_live(columns, counts, k, e):
    slots, rows = columns.shape
    row_index = lax.axis_index("col") * rows + k
    all_rows = rows * lax.axis_size("col")
    return lax.rem(e - row_index + all_rows * slots, slots) < counts[k]


class Plan:
    def __init__(self, ref, rows, slots, shards):
        self.ref, self.rows, self.slots, self.shards = ref, rows, slots, shards
        self.lens = rows * slots * shards
        self.loads = self.lens + slots * shards
        self.size = self.loads + SLAB_DEV * shards

    def entry(self, place, shard, j):
        return (place * self.shards + shard) * self.rows + j

    def length(self, place, shard):
        return self.lens + place * self.shards + shard

    def load(self, column):
        return self.loads + column


def plan_of(ref, operand):
    rows = operand.shape[1] // SIDE
    return Plan(ref, rows, lax.axis_size("row"), lax.axis_size("col"))


def begin(ny, which, columns, counts, operand, own, twin, plan_ref, operand_near, own_near, total, sems):
    copies = [
        pltpu.make_async_copy(far, near, sems.at[j])
        for j, (far, near) in enumerate(((operand, operand_near), (own, own_near)))
    ]
    for copy in copies:
        copy.start()
    slots, rows = columns.shape
    plan = plan_of(plan_ref, operand)

    def clear(j, carry):
        plan_ref[plan.lens + j] = 0
        return carry

    lax.fori_loop(0, plan.size - plan.lens, clear, 0)
    for place in range(slots):
        e = slot_of(place, ny)

        def one(k, carry, place=place, e=e):
            @pl.when(is_live(columns, counts, k, e))
            def _():
                column = columns[e, k]
                plan_ref[plan.load(column)] = plan_ref[plan.load(column)] + 1
                shard = lax.div(column, SLAB_DEV)
                at = plan.length(place, shard)
                length = plan_ref[at]
                plan_ref[plan.entry(place, shard, length)] = k * SLAB_DEV + column - shard * SLAB_DEV
                plan_ref[at] = length + 1

            return carry

        lax.fori_loop(0, rows, one, 0)
    for copy in copies:
        copy.wait()
    total[...] = jnp.zeros_like(total)

    @pl.when(jnp.logical_not(is_inner()))
    def _():
        for place, held in enumerate((own_near, twin)):
            add_terms(plan, which(lax.axis_index("col")), place, held, total, operand_near)


def add_terms(plan, shard, place, held, total, operand):
    length = plan.ref[plan.length(place, shard)]

    def term(j):
        entry = jnp.where(j < length, plan.ref[plan.entry(place, shard, jnp.minimum(j, plan.rows - 1))], 0)
        k, column = lax.div(entry, SLAB_DEV), lax.rem(entry, SLAB_DEV)
        block = held[k, 0]
        block = jnp.where(j < length, block, jnp.zeros_like(block))
        left = operand[:, pl.ds(pl.multiple_of(k * SIDE, SIDE), SIDE)]
        lanes = pl.ds(pl.multiple_of(column * SIDE, SIDE), SIDE)
        return lanes, jnp.dot(left, block, preferred_element_type=jnp.float32)

    def step(some, carry):
        for lanes, value in [term(ABREAST * some + j) for j in range(ABREAST)]:
            total[:, lanes] = total[:, lanes] + value
        return carry

    lax.fori_loop(0, lax.div(length + ABREAST - 1, ABREAST), step, 0)


def go_on(which, place, plan_ref, operand, held, _, total):
    @pl.when(jnp.logical_not(is_inner()))
    def _():
        add_terms(plan_of(plan_ref, operand), which(lax.axis_index("col")), place, held, total, operand)


def code_sum(which, place, plan_ref, operand, held, total, out):
    plan = plan_of(plan_ref, operand)
    shard = which(lax.axis_index("col"))

    @pl.when(is_inner())
    def _():
        out[...] = jnp.zeros_like(out)

    @pl.when(jnp.logical_not(is_inner()))
    def _():
        add_terms(plan, shard, place, held, total, operand)
        values = [(b, lambda b=b: total[:, lanes_of(b)]) for b in range(SLAB_DEV)]
        put_coded([(out, ALL)], values, counts_of(plan, shard))


def fill(slab, plan, shard, blocks):
    slab[...] = jnp.zeros_like(slab)
    for place, held in enumerate(blocks):

        def one(j, carry, place=place, held=held):
            entry = plan.ref[plan.entry(place, shard, j)]
            k, column = lax.div(entry, SLAB_DEV), lax.rem(entry, SLAB_DEV)
            where = (pl.ds(pl.multiple_of(k * SIDE, SIDE), SIDE), pl.ds(pl.multiple_of(column * SIDE, SIDE), SIDE))
            slab[where] = held[k, 0]
            return carry

        lax.fori_loop(0, plan.ref[plan.length(place, shard)], one, 0)


def counts_of(plan, shard):
    row = lax.broadcasted_iota(jnp.int32, (HEAD, SIDE), 0)
    head = jnp.zeros((HEAD, SIDE), jnp.int32)
    for b in range(SLAB_DEV):
        head = jnp.where(row == SLAB_DEV + b, plan.ref[plan.load(shard * SLAB_DEV + b)], head)
    return head


def tiles(width, body):
    def step(tile, carry):
        body(tile, pl.ds(pl.multiple_of(tile * TILE, TILE), TILE))
        return carry

    lax.fori_loop(0, width // TILE, step, 0)


def coded_product(which, helds, nblocks, plan_ref, operand, *refs):
    blocks, (*outs, slab) = refs[:nblocks], refs[nblocks:]
    plan = plan_of(plan_ref, operand)
    shard = which(lax.axis_index("col"))
    fill(slab, plan, shard, blocks)
    done = {}

    def values(block):
        tile, at = block * SIDE // TILE, block * SIDE % TILE
        if tile not in done:
            lanes = pl.ds(tile * TILE, TILE)
            done[tile] = jnp.dot(operand[...], slab[:, lanes], preferred_element_type=jnp.float32)
        return done[tile][:, at : at + SIDE]

    put_coded(list(zip(outs, helds)), [(b, functools.partial(values, b)) for b in ALL], counts_of(plan, shard))


def plain_products(plain, nblocks, plan_ref, operand, *refs):
    blocks, (*outs, slab) = refs[:nblocks], refs[nblocks:]
    outs, loads = outs[: len(plain)], outs[len(plain) :]
    plan = plan_of(plan_ref, operand)
    for which, out, row in zip(plain, outs, loads):
        shard = which(lax.axis_index("col"))
        fill(slab, plan, shard, blocks)

        def body(tile, lanes, out=out):
            out[:, lanes] = jnp.dot(operand[...], slab[:, lanes], preferred_element_type=jnp.float32)

        tiles(slab.shape[1], body)
        row[...] = counts_of(plan, shard)


def relay(part, own, own_load, came, out):
    inner = is_inner()
    held, rows = blocks_of(part), own.shape[0]

    @pl.when(inner)
    def _():
        head = head_of(came)
        values = [
            (b, lambda at=at, b=b: own[:, lanes_of(b)] + decode(came, head, at, rows)) for at, b in enumerate(held)
        ]
        put_coded([(out, held)], values, own_load[...] + head)

    @pl.when(jnp.logical_not(inner))
    def _():
        put_coded([(out, held)], [(b, lambda b=b: own[:, lanes_of(b)]) for b in held], own_load[...])


def settle(own, own_load, *refs):
    *came_a, came_b, came_f, out, out_load = refs
    rows = own.shape[0]

    @pl.when(is_inner())
    def _():
        head_b, head_f = head_of(came_b), head_of(came_f)
        out_load[...] = own_load[...] + head_b + head_f
        for b in ALL:
            came = decode(came_b, head_b, b, rows) + decode(came_f, head_f, b, rows)
            out[:, lanes_of(b)] = own[:, lanes_of(b)] + came

    @pl.when(jnp.logical_not(is_inner()))
    def _():
        out_load[...] = own_load[...] + head_of(came_a[0])
        for part, came in enumerate(came_a):
            head = head_of(came)
            for at, b in enumerate(blocks_of(part)):
                out[:, lanes_of(b)] = own[:, lanes_of(b)] + decode(came, head, at, rows)


def inflate(part, own, came, out, totals):
    rows, head = own.shape[0], head_of(came)
    for at, b in enumerate(blocks_of(part)):
        expanded = own[:, lanes_of(b)] + decode(came, head, at, rows)
        inflated = expanded * expanded
        out[:, lanes_of(at)] = inflated
        totals[:, lanes_of(at)] = jnp.sum(inflated.reshape(-1, 8, SIDE), axis=0)


def count(own_load, came, load):
    head = own_load[...] + head_of(came)
    for j in range(SLAB_DEV):
        load[j] = jnp.max(head[SLAB_DEV + j : SLAB_DEV + j + 1])


def scale(all_rows, part, inflated, *refs):
    *totals, out, scaled, sems = refs[:-4] + refs[-3:] if part else refs
    rows, width = inflated.shape
    total = totals[0][...]
    for other in totals[1:]:
        total = total + other[...]
    total = jnp.sum(total, axis=0, keepdims=True)
    factor = 1.0 / (total / all_rows + 1e-06)
    few = rows // sems.shape[0]
    copies = []
    for j in range(sems.shape[0]):
        these = pl.ds(j * few, few)
        scaled[these, :] = inflated[these, :] * factor
        copy = pltpu.make_async_copy(scaled.at[these, :], out.at[these, pl.ds(part * width, width)], sems.at[j])
        copy.start()
        copies.append(copy)
    for copy in copies:
        copy.wait()


def call(kernel, ins, out_shape, out_specs, scratch=(), flops=0, few=0, far=0, onto=None, last=False):
    moved = sum(x.size * x.dtype.itemsize for x in list(ins) + list(out_shape))
    return pl.pallas_call(
        kernel,
        in_specs=[SMEM] * few + [pl.BlockSpec(memory_space=pltpu.HBM)] * far + [VMEM] * (len(ins) - few - far - last) + [pl.BlockSpec(memory_space=pl.ANY)] * last,
        out_shape=out_shape,
        out_specs=out_specs,
        scratch_shapes=list(scratch),
        input_output_aliases=onto or {},
        compiler_params=pltpu.CompilerParams(vmem_limit_bytes=24 << 20),
        cost_estimate=pl.CostEstimate(flops=flops // COST, bytes_accessed=moved // COST, transcendentals=0),
    )(*ins)


def body_line(operand_panel, slot_blocks, slot_columns, live_counts):
    ny = lax.axis_size("row") // 2
    rows, depth = operand_panel.shape
    here, slots = slot_columns.shape
    width = SLAB_DEV * SIDE
    shards = lax.axis_size("col")
    f32 = functools.partial(jax.ShapeDtypeStruct, dtype=jnp.float32)
    i32 = functools.partial(jax.ShapeDtypeStruct, dtype=jnp.int32)
    coded = jax.ShapeDtypeStruct((SLAB_DEV * rows + HEAD, SIDE), jnp.int16)

    swap = [(a, a ^ 1) for a in range(2 * ny)]

    def turn(by):
        return [(a, ((a // 2 + by) % ny) * 2 + a % 2) for a in range(2 * ny)]

    def first(z):
        return jnp.where(z == 0, 2, 1)

    def second(z):
        return jnp.where(lax.rem(z, 2) == 0, 3, 0)

    def inner(z):
        return jnp.where(z < 2, 2, 1)

    def third(z):
        return jnp.where(z == 0, 1, jnp.where(z == 1, 3, jnp.where(z == 2, 0, 2)))

    flops = 2 * rows * depth * width
    turned = [lax.ppermute(slot_blocks, "row", turn(by)) for by in range(1, ny)]
    twin = lax.ppermute(slot_blocks, "row", swap)
    plan, operand_near, own_near, total = call(
        functools.partial(begin, ny, first),
        [slot_columns.T, live_counts, operand_panel, slot_blocks, twin],
        [
            i32((Plan(None, here, slots, shards).size,)),
            jax.ShapeDtypeStruct(operand_panel.shape, operand_panel.dtype),
            jax.ShapeDtypeStruct(slot_blocks.shape, slot_blocks.dtype),
            f32((rows, width)),
        ],
        [SMEM] + [VMEM] * 3,
        [pltpu.SemaphoreType.DMA((2,))],
        flops // 4,
        few=2,
        far=2,
    )
    turned, plan = lax.optimization_barrier((turned, plan))
    blocks = [own_near, twin]
    blocks += [x for came in turned for x in (came, lax.ppermute(came, "row", swap))]
    for place in range(2, slots - 1):
        [total] = call(
            functools.partial(go_on, first, place),
            [plan, operand_near, blocks[place], total],
            [f32((rows, width))],
            [VMEM],
            (),
            flops // 8,
            1,
            onto={3: 0},
        )
    [send_f] = call(
        functools.partial(code_sum, first, slots - 1),
        [plan, operand_near, blocks[-1], total],
        [coded],
        [VMEM],
        (),
        flops // 8,
        1,
    )
    came_f = lax.ppermute(send_f, "col", [(0, 2), (1, 0), (2, 3), (3, 1)])
    ins = [plan, operand_near, *blocks]
    slab = [pltpu.VMEM((depth, width), jnp.bfloat16)]
    part_coded = jax.ShapeDtypeStruct((SLAB_DEV // PARTS * rows + HEAD, SIDE), jnp.int16)
    send_a = call(
        functools.partial(coded_product, second, [blocks_of(j) for j in range(PARTS)], len(blocks)),
        ins,
        [part_coded] * PARTS,
        [VMEM] * PARTS,
        slab,
        flops,
        1,
    )
    came_a = [lax.ppermute(one, "col", [(0, 1), (1, 0), (2, 3), (3, 2)]) for one in send_a]
    [send_b] = call(
        functools.partial(coded_product, inner, [ALL], len(blocks)), ins, [coded], [VMEM], slab, flops, 1
    )
    came_b = lax.ppermute(
        send_b,
        ("row", "col"),
        [(4 * r + c, 4 * r + 3 - c if c in (1, 2) else 4 * (r ^ 1) + c) for r in range(2 * ny) for c in range(4)],
    )
    ins[0], came_f = lax.optimization_barrier((ins[0], came_f))
    passed, own, passed_load, own_load = call(
        functools.partial(plain_products, (third, lambda z: z), len(blocks)),
        ins,
        [f32((rows, width)), f32((rows, width)), i32((HEAD, SIDE)), i32((HEAD, SIDE))],
        [VMEM] * 4,
        slab,
        2 * flops,
        1,
    )
    came_a[-1], came_b = lax.optimization_barrier((came_a[-1], came_b))
    came_t = []
    for part in range(PARTS):
        [send_t] = call(
            functools.partial(relay, part), [passed, passed_load, came_a[part]], [part_coded], [VMEM]
        )
        came_t.append(lax.ppermute(send_t, "col", [(0, 1), (1, 3), (3, 2), (2, 0)]))
    own, own_load = call(
        settle, [own, own_load, *came_a, came_b, came_f], [f32((rows, width)), i32((HEAD, SIDE))], [VMEM] * 2
    )
    all_rows = rows * lax.axis_size("row")
    hbm = pl.BlockSpec(memory_space=pl.ANY)
    result = []
    [load] = call(count, [own_load, came_t[0]], [i32((SLAB_DEV,))], [SMEM])
    for part in range(PARTS):
        inflated, totals = call(
            functools.partial(inflate, part),
            [own, came_t[part]],
            [f32((rows, width // PARTS)), f32((8, width // PARTS))],
            [VMEM] * 2,
        )
        others = [totals]
        steps = [(by, 1) for by in range(1, ny)] + [(by, 0) for by in range(1, ny)] + [(0, 1)]
        for by, flip in steps:
            pairs = [(a, ((a // 2 + by) % ny) * 2 + (a % 2 ^ flip)) for a in range(2 * ny)]
            others.append(lax.ppermute(totals, "row", pairs))
        result = call(
            functools.partial(scale, all_rows, part),
            [inflated, *others, *result],
            [f32((rows, width))],
            [hbm],
            [pltpu.VMEM((rows, width // PARTS), jnp.float32), pltpu.SemaphoreType.DMA((4,))],
            onto={1 + len(others): 0} if part else None,
            last=bool(part),
        )
    return result[0], load


def densify(blocks, columns, counts, first_row, slab_width):
    rows_here, slots = columns.shape
    side = blocks.shape[2]
    places = jnp.arange(slots, dtype=jnp.int32)
    rows_index = first_row + jnp.arange(rows_here, dtype=jnp.int32)
    live = jnp.mod(places[None, :] - rows_index[:, None], slots) < counts[:, None]
    onehot = (columns[:, :, None] == jnp.arange(slab_width, dtype=jnp.int32)[None, None, :]) & live[:, :, None]
    dense = jnp.einsum(
        "kej,kebc->kbjc", onehot.astype(jnp.bfloat16), blocks, preferred_element_type=jnp.float32
    )
    dense = dense.astype(jnp.bfloat16).reshape(rows_here * side, slab_width * side)
    return (dense, jnp.sum(onehot.astype(jnp.float32), axis=(0, 1)))


def body_any(operand_panel, slot_blocks, slot_columns, live_counts):
    gathered = lax.all_gather(slot_blocks, "row", axis=1, tiled=True)
    slab_width = SLAB_DEV * lax.axis_size("col")
    first_row = lax.axis_index("col") * slot_columns.shape[0]
    dense, load = densify(gathered, slot_columns, live_counts, first_row, slab_width)
    partial_terms = jnp.dot(operand_panel, dense, preferred_element_type=jnp.float32)
    expanded, load_mine = (
        lax.psum_scatter(partial_terms, "col", scatter_dimension=1, tiled=True),
        lax.psum_scatter(load, "col", scatter_dimension=0, tiled=True),
    )
    inflated = expanded * expanded
    totals = lax.psum(jnp.sum(inflated, axis=0), "row")
    all_rows = expanded.shape[0] * lax.axis_size("row")
    mcl_columns = inflated / (totals / all_rows + 1e-06)
    return (mcl_columns, load_mine.astype(jnp.int32))


def solution(mesh):
    placed = (
        P(("groups", "row"), "col"),
        P(("groups", "col"), "row", None, None),
        P(("groups", "col"), None),
        P(("groups", "col")),
    )
    return jax.shard_map(
        body_line if mesh.shape["col"] == 4 else body_any,
        mesh=mesh,
        in_specs=placed,
        out_specs=(P(("groups", "row"), "col"), P(("groups", "col"))),
        check_vma=False,
    )
```
